512 devices in a mesh: arcs: 128 (over x, z, core), coef: 4 (over y).
Axes of the slice: x: 4, y: 4, z: 16, core: 2. Of those that a mesh axis runs over, the one named last changes fastest.
Arguments:
- design: bfloat16 [16384, 9728], P('arcs', 'coef'), as said below
- observed: bfloat16 [16384, 64], P('arcs'), may hold values from -6 to 6
- arc_lengths: int32 [128, 4], P('arcs'), may hold values from 1 to 64, as said below
- arc_months: int32 [128, 4], P('arcs'), may hold values from 0 to 1
- walk_weight: float32 [9728], P('coef'), may hold values from 0.1 to 2
Outputs:
- solution: float32 [9728, 128], P('coef')
The draws below stay inside these ranges and needn't reach their ends.
Inputs may be any that keep to these rules, and one draw needn't show every extreme that they name: `arc_lengths`: on each index of arcs the arcs fill the first rows one after another; their lengths sum to at most 128 there, and to exactly 128 on some index; no arc is longer than 64 and some arc has exactly that length. `design`: rows and columns have unequal scales.
All inputs are finite; a program needn't handle non-finite values.
Results may differ from the reference program's by a relative error of at most 0.0019.
Values may be sent and summed in bfloat16 or wider, within the bound.
A program may use at most 64 MiB of HBM per device.

```python
import math
import jax
import jax.numpy as jnp
from jax import lax

NCOEF = 9405
K = 64
ROWS_DEV = 128
ARCS_DEV = 4
ITERS = 2
NPAD = 9728
NROWS = 16384
N_ARCS = 128


def draw_design(key, part):
    key = jax.random.fold_in(key, 23)
    key_rows, key_cols, key_noise = jax.random.split(key, 3)
    total_rows = N_ARCS * ROWS_DEV
    row_scale = jnp.exp(jax.random.uniform(key_rows, (total_rows, 1), jnp.float32, 0.0, math.log(10.0)))
    col_scale = jnp.exp(jax.random.uniform(key_cols, (1, NPAD), jnp.float32, 0.0, math.log(10.0)))
    factor = 0.1 / math.sqrt(total_rows)
    values = jax.random.normal(key_noise, (total_rows, NPAD), jnp.float32) * row_scale * col_scale * factor
    return values.astype(jnp.bfloat16)


def split_rows(total, weights):
    count = weights.shape[1]
    running = jnp.cumsum(weights, axis=1)
    edges = (total[:, None] - count) * running // running[:, -1:]
    before = jnp.concatenate([jnp.zeros((weights.shape[0], 1), jnp.int32), edges[:, :-1]], axis=1)
    return (edges - before + 1).astype(jnp.int32)


def draw_arc_lengths(key, part):
    key = jax.random.fold_in(key, 11)
    key_expo, key_shrink, key_full, key_weights = jax.random.split(key, 4)
    expo = jax.random.randint(key_expo, (N_ARCS,), 1, 4)
    shrink = jax.random.randint(key_shrink, (N_ARCS,), 0, ROWS_DEV // 32 + 1)
    fullest = jax.random.randint(key_full, (), 0, N_ARCS)
    live = ROWS_DEV // jnp.left_shift(jnp.ones((N_ARCS,), jnp.int32), expo) - shrink
    weights = jax.random.randint(key_weights, (N_ARCS, ARCS_DEV), 1, 8)
    drawn = split_rows(live, weights)
    half = ROWS_DEV // 2
    rest_total = jnp.full((N_ARCS,), ROWS_DEV - half, jnp.int32)
    rest = split_rows(rest_total, weights[:, 1:])
    full_row = jnp.concatenate([jnp.full((N_ARCS, 1), half, jnp.int32), rest], axis=1)
    chosen = jnp.where((jnp.arange(N_ARCS) == fullest)[:, None], full_row, drawn)
    return chosen.astype(jnp.int32)


def with_ends(values, key, low, largest):
    longest = values.shape.index(max(values.shape))
    spots = []
    for shift in (0, 1):
        where = [jax.random.randint(jax.random.fold_in(key, axis), (), 0, length) for axis, length in enumerate(values.shape)]
        where[longest] = (where[longest] + shift) % values.shape[longest]
        spots.append(tuple(where))
    return values.at[spots[0]].set(low).at[spots[1]].set(largest)


def steps_of(rng, shape, cuts, smallest, high):
    loudness = 1.0
    for dim, shards_of in cuts:
        draws = jax.random.uniform(jax.random.fold_in(jax.random.fold_in(rng, 6), dim), (shards_of,), jnp.float32, smallest / len(cuts), high / len(cuts))
        loudness = loudness * jnp.repeat(jnp.exp(draws), shape[dim] // shards_of).reshape((-1,) + (1,) * (len(shape) - 1 - dim))
    return loudness


def scatter_about(own_key, dims, deviation, limit, pieces=(), held_as=jnp.bfloat16):
    result = deviation * jax.random.normal(own_key, dims, jnp.float32)
    if pieces:
        result = result * steps_of(own_key, dims, pieces, -0.22, 0.18)
    return jnp.clip(result, -limit, limit).astype(held_as)


def setup_inputs(seed: int = 0) -> dict:
    seeds = jax.random.split(jax.random.key(seed), 6)
    return {
        "design": draw_design(jax.random.fold_in(seeds[5], 71), 0),
        "observed": scatter_about(seeds[1], (NROWS, K), 1.0, 6.0, ((0, 128),)),
        "arc_lengths": draw_arc_lengths(jax.random.fold_in(seeds[5], 71), 0),
        "arc_months": with_ends(jax.random.randint(seeds[3], (N_ARCS, ARCS_DEV), 0, 2), jax.random.fold_in(seeds[3], 1), 0, 1).astype(jnp.int32),
        "walk_weight": jnp.clip(jnp.exp(math.log(2.0) - 2.9957323 * jax.random.uniform(seeds[4], (NPAD,), jnp.float32) ** steps_of(seeds[4], (NPAD,), ((0, 4),), -0.2, 0.2)), 0.1, 2.0),
    }


epsilon = 1e-06

def fold_months(values, width):
    return values[:width] + values[width:]

def paired(values):
    return jnp.concatenate([values, values])[None, :]

def reference(design, observed, arc_lengths, arc_months, walk_weight):
    width = observed.shape[1]
    ends = jnp.cumsum(arc_lengths, axis=1)
    starts = ends - arc_lengths
    positions = jnp.arange(ROWS_DEV, dtype=jnp.int32)
    inside = (positions[None, None, :] >= starts[:, :, None]) & (positions[None, None, :] < ends[:, :, None])
    month_row = lax.optimization_barrier(jnp.sum(jnp.where(inside, arc_months[:, :, None], 0), axis=1)).reshape(-1)
    is_live = jnp.any(inside, axis=1).reshape(-1)
    month_side = (jnp.arange(2 * width, dtype=jnp.int32) >= width).astype(jnp.int32)
    mask_stack = jnp.where(is_live[:, None] & (month_row[:, None] == month_side[None, :]), 1.0, 0.0).astype(jnp.float32)
    col_mask = (jnp.arange(NPAD, dtype=jnp.int32) < NCOEF).astype(jnp.float32)[:, None]
    arc_blocks = design.reshape(N_ARCS, ROWS_DEV, NPAD)
    walk_col = walk_weight[:, None]

    def forward(vec_raw):
        rounded = vec_raw.astype(jnp.bfloat16)
        images = lax.map(lambda one_block: jnp.dot(one_block, rounded, preferred_element_type=jnp.float32), arc_blocks)
        return images.reshape(N_ARCS * ROWS_DEV, 2 * width) * mask_stack

    def adjoint(obs_raw):
        rounded = obs_raw.astype(jnp.bfloat16).reshape(N_ARCS, ROWS_DEV, 2 * width)

        def add_block(carry, pair_in):
            one_block, rows_in = pair_in
            product = lax.dot_general(one_block, rows_in, (((0,), (0,)), ((), ())), preferred_element_type=jnp.float32)
            return (carry + product, None)
        total, _ = lax.scan(add_block, jnp.zeros((NPAD, 2 * width), jnp.float32), (arc_blocks, rounded))
        return total * col_mask
    obs_raw = jnp.concatenate([observed, observed], axis=1).astype(jnp.float32) * mask_stack
    beta_norm = jnp.sqrt(fold_months(lax.optimization_barrier(jnp.sum(obs_raw * obs_raw, axis=0)), width) + epsilon)
    vec_raw = adjoint(obs_raw) / paired(beta_norm)
    alpha_norm = jnp.sqrt(fold_months(lax.optimization_barrier(jnp.sum(vec_raw * vec_raw, axis=0)), width) + epsilon)
    vec_unit = vec_raw / paired(alpha_norm)
    obs_unit = obs_raw / paired(beta_norm)
    walk_unit = jnp.zeros((NPAD, width), jnp.float32)
    search_dir = vec_unit
    phi_bar = beta_norm
    rho_bar = alpha_norm
    solution = jnp.zeros((NPAD, 2 * width), jnp.float32)
    for step in range(ITERS):
        obs_raw = forward(vec_raw) / paired(alpha_norm) - paired(alpha_norm) * obs_unit
        walk_raw = walk_col * (vec_unit[:, width:] - vec_unit[:, :width]) - alpha_norm[None, :] * walk_unit
        beta_norm = jnp.sqrt(fold_months(lax.optimization_barrier(jnp.sum(obs_raw * obs_raw, axis=0)), width) + lax.optimization_barrier(jnp.sum(walk_raw * walk_raw, axis=0)) + epsilon)
        rho_now = jnp.sqrt(rho_bar * rho_bar + beta_norm * beta_norm)
        rot_cos = rho_bar / rho_now
        rot_sin = beta_norm / rho_now
        phi_step = rot_cos * phi_bar
        phi_bar = rot_sin * phi_bar
        solution = solution + paired(phi_step / rho_now) * search_dir
        if step + 1 < ITERS:
            obs_unit = obs_raw / paired(beta_norm)
            walk_unit = walk_raw / beta_norm[None, :]
            walk_back = jnp.concatenate([-walk_col * walk_unit, walk_col * walk_unit], axis=1)
            vec_raw = adjoint(obs_raw) / paired(beta_norm) + walk_back - paired(beta_norm) * vec_unit
            alpha_norm = jnp.sqrt(fold_months(lax.optimization_barrier(jnp.sum(vec_raw * vec_raw, axis=0)), width) + epsilon)
            vec_unit = vec_raw / paired(alpha_norm)
            rho_bar = -rot_cos * alpha_norm
            search_dir = vec_unit - paired(rot_sin * alpha_norm / rho_now) * search_dir
    return solution
```

```python
import functools

import jax
import jax.numpy as jnp
from jax import lax
from jax.experimental import pallas as pl
from jax.experimental.pallas import tpu as pltpu
from jax.sharding import PartitionSpec as P

NCOEF = 9405
EPS = 1e-06
MESH = pl.DeviceIdType.MESH
NX, NZ, NC, NY = 4, 16, 2, 4
TILE = 16
F32, BF16 = jnp.float32, jnp.bfloat16


def kernel(
    design, observed, lengths, months, walk, out,
    d_ref, dt, wt, mask_ref, u_ref, bc_ref,
    cs, cr, xs, xr, tb, zr, own, vh, vl, yb, ny, nc, nx, nz,
    d_sem, cs_s, cs_r, xs_s, xs_r, zs_s, zs_r,
    az_s, az_r, ax_s, ax_r, ac_s, ac_r, y_s, y_r, ny_s, ny_r,
    nc_s, nc_r, nx_s, nx_r, nz_s, nz_r,
):
    rows = d_ref.shape[0]
    columns = d_ref.shape[1]
    tiles = columns // (NC * NX * TILE)
    piece = tiles * TILE
    extras = tiles - NZ
    arc, y = lax.axis_index("arcs"), lax.axis_index("coef")
    core = lax.rem(arc, NC)
    z = lax.rem(arc // NC, NZ)
    x = arc // (NC * NZ)

    def at(x_, z_, c_):
        return ((x_ * NZ + z_) * NC + c_, y)

    def wrap(v, n):
        return lax.rem(v, n)

    sibling = at(x, z, 1 - core)
    hops4 = (2, 1, 3)

    def x_peer(d):
        return wrap(x + d, NX)

    def y_peer(d):
        return (arc, wrap(y + d, NY))

    def extra_owner(e, c_):
        return 5 * e + 3 * c_

    drains = []

    def push(src, dst, ssem, rsem, dev):
        return pltpu.make_async_remote_copy(
            src_ref=src, dst_ref=dst, send_sem=ssem, recv_sem=rsem,
            device_id=dev, device_id_type=MESH,
        )

    def go(copy):
        copy.start()
        drains.append(copy.wait_send)

    def over_z(body):
        def step(d, _):
            body(wrap(z + d, NZ))
            return 0
        lax.fori_loop(1, NZ, step, 0)

    load = pltpu.make_async_copy(design, d_ref, d_sem)
    load.start()

    barrier = pltpu.get_barrier_semaphore()

    def greet(dev):
        pl.semaphore_signal(barrier, inc=1, device_id=dev, device_id_type=MESH)

    greet(sibling)
    for d in hops4:
        greet(at(x_peer(d), z, core))
        greet(y_peer(d))
    over_z(lambda z_: greet(at(x, z_, core)))

    lane = lax.broadcasted_iota(jnp.int32, (rows, 128), 1)
    row = lax.broadcasted_iota(jnp.int32, (rows, 128), 0)
    start = jnp.int32(0)
    month_row = jnp.full((rows, 128), -1, jnp.int32)
    for j in range(lengths.shape[1]):
        end = start + lengths[0, j]
        month_row = jnp.where((row >= start) & (row < end), months[0, j], month_row)
        start = end
    side = (lane >= 64).astype(jnp.int32)
    mask_stack = (month_row == side).astype(F32)
    mask_ref[...] = mask_stack
    half = rows // 2
    low = lax.broadcasted_iota(jnp.int32, (half, 128), 1) < 64
    ob = observed[...].astype(F32)
    ob = jnp.concatenate([ob, ob], axis=1) * mask_stack

    def turn(v):
        return pltpu.roll(v, 64, 1)

    def compact(v):
        s = v + turn(v)
        return jnp.where(low, s[:half], s[half:])

    def expand(v):
        t = turn(v)
        first = jnp.where(low, v, t)
        second = jnp.where(low, t, v)
        return (jnp.concatenate([first, second], axis=0) * mask_ref[...]).astype(BF16)

    def fold(v):
        return v + turn(jnp.broadcast_to(v, (8, 128)))[:1]

    def total(v):
        return jnp.sum(v, axis=0, keepdims=True)

    def padded(parts):
        rest = 4 - len(parts)
        if rest:
            parts = parts + [jnp.zeros((rest, 128), F32)]
        return jnp.concatenate(parts, axis=0)

    bc = compact(ob)
    bc_ref[...] = bc
    u_ref[0] = expand(bc)

    has_extra = jnp.int32(0)
    which = jnp.int32(0)
    for e in range(extras):
        hit = (z == extra_owner(e, core)).astype(jnp.int32)
        has_extra = has_extra + hit
        which = which + e * hit
    base = (core * NX + x) * piece
    tile_of = (z, NZ + which)
    row16 = lax.broadcasted_iota(jnp.int32, (TILE, 128), 0)
    w_parts, keep_parts = [], []
    for s in range(2):
        first = base + tile_of[s] * TILE
        block = first // 128
        inside = first - block * 128
        strip = walk[0:1, pl.ds(pl.multiple_of(block * 128, 128), 128)]
        wt[s] = jnp.broadcast_to(strip, (128, 128)).T
        w_parts.append(wt[s, pl.ds(pl.multiple_of(inside, TILE), TILE), :])
        keep = (y * columns + first + row16) < NCOEF
        if s == 1:
            keep = keep & (jnp.full((TILE, 128), has_extra, jnp.int32) > 0)
        keep_parts.append(keep.astype(F32))
    w_own = jnp.concatenate(w_parts, axis=0)
    keep_own = jnp.concatenate(keep_parts, axis=0)

    load.wait()
    for j in range(columns // 128):
        dt[j * 128:(j + 1) * 128, :] = d_ref[:, j * 128:(j + 1) * 128].T
    pl.semaphore_wait(barrier, 1 + 2 * len(hops4) + NZ - 1)

    def n_core(k, value):
        nc[k, core] = value
        go(push(nc.at[k, core], nc.at[k, core], nc_s.at[k], nc_r.at[k], sibling))

    def n_core_sum(k):
        push(nc.at[k, core], nc.at[k, 1 - core], nc_s.at[k], nc_r.at[k], sibling).wait_recv()
        return nc[k, 0] + nc[k, 1]

    def n_x(k, value):
        nx[k, x] = value
        for d in hops4:
            x_ = x_peer(d)
            go(push(nx.at[k, x], nx.at[k, x], nx_s.at[k, x_], nx_r.at[k, x], at(x_, z, core)))

    def n_x_sum(k):
        for d in hops4:
            x_ = x_peer(d)
            push(nx.at[k, x], nx.at[k, x_], nx_s.at[k, x_], nx_r.at[k, x_], at(x_, z, core)).wait_recv()
        return (nx[k, 0] + nx[k, 1]) + (nx[k, 2] + nx[k, 3])

    def n_z_copy(k, z_):
        return push(nz.at[k, z], nz.at[k, z], nz_s.at[k, z_], nz_r.at[k, z], at(x, z_, core))

    def n_z(k, value):
        nz[k, z] = value
        over_z(lambda z_: n_z_copy(k, z_).start())
        drains.append(lambda: over_z(lambda z_: n_z_copy(k, z_).wait_send()))

    def n_z_sum(k):
        over_z(lambda z_: push(
            nz.at[k, z], nz.at[k, z_], nz_s.at[k, z_], nz_r.at[k, z_], at(x, z_, core)).wait_recv())
        return jnp.sum(nz[k], axis=0)

    def adjoint_piece(r, h, p):
        first = pl.multiple_of((h * NX + p) * piece, TILE)
        value = jnp.dot(dt[pl.ds(first, piece), :], u_ref[r], preferred_element_type=F32)
        return value.reshape(tiles, TILE, 128)

    def reduce_scatter(r, k, norm_value):
        n_core(k, norm_value)
        order = [x_peer(d) for d in hops4] + [x]

        def core_copy(p):
            return push(cs.at[r, p], cr.at[r, p], cs_s.at[r, p], cs_r.at[r, p], sibling)

        for p in order:
            cs[r, p] = adjoint_piece(r, 1 - core, p)
            go(core_copy(p))
        for i, p in enumerate(order):
            mine = adjoint_piece(r, core, p)
            core_copy(p).wait_recv()
            mine = mine + cr[r, p]
            if i < 3:
                xs[r, p] = mine
                go(push(xs.at[r, p], xr.at[r, x], xs_s.at[r, p], xs_r.at[r, x], at(p, z, core)))
            else:
                xr[r, x] = mine
            if i == 0:
                n_x(k, n_core_sum(k))
        for p in order[:3]:
            push(xs.at[r, p], xr.at[r, p], xs_s.at[r, p], xs_r.at[r, p], at(p, z, core)).wait_recv()
        tb[r] = (xr[r, 0] + xr[r, 1]) + (xr[r, 2] + xr[r, 3])

        def main_copy(z_, src):
            return push(tb.at[r, z_], zr.at[r, 0, src], zs_s.at[r, 0, z_], zs_r.at[r, 0, src], at(x, z_, core))

        def extra_copy(e, src):
            z_ = extra_owner(e, core)
            return push(tb.at[r, NZ + e], zr.at[r, 1, src], zs_s.at[r, 1, z_], zs_r.at[r, 1, src], at(x, z_, core))

        over_z(lambda z_: main_copy(z_, z).start())
        for e in range(extras):
            @pl.when(z != extra_owner(e, core))
            def _():
                extra_copy(e, z).start()
        n_z(k, n_x_sum(k))
        zr[r, 0, z] = tb[r, z]
        over_z(lambda z_: main_copy(z_, z_).wait_recv())
        own[r, 0] = jnp.sum(zr[r, 0], axis=0)
        own[r, 1] = jnp.zeros((TILE, 128), F32)

        @pl.when(has_extra > 0)
        def _():
            zr[r, 1, z] = tb[r, NZ + which]
            over_z(lambda z_: push(
                tb.at[r, NZ], zr.at[r, 1, z_], zs_s.at[r, 1, z_], zs_r.at[r, 1, z_], at(x, z_, core)).wait_recv())
            own[r, 1] = jnp.sum(zr[r, 1], axis=0)

        def drain():
            over_z(lambda z_: main_copy(z_, z).wait_send())
            for e in range(extras):
                @pl.when(z != extra_owner(e, core))
                def _():
                    extra_copy(e, z).wait_send()
        drains.append(drain)
        norm = n_z_sum(k)
        return own[r].reshape(2 * TILE, 128) * keep_own, norm

    def gz_main(v, r, q, src, z_):
        ref = v.at[r, core, x, src]
        return push(ref, ref, az_s.at[q, 0, z_], az_r.at[q, 0, src], at(x, z_, core))

    def gz_extra(v, r, q, e, z_):
        ref = v.at[r, core, x, NZ + e]
        return push(ref, ref, az_s.at[q, 1, z_], az_r.at[q, 1, e], at(x, z_, core))

    def gather_z_start(v, r, q, value):
        v[r, core, x, z] = value[:TILE]
        over_z(lambda z_: gz_main(v, r, q, z, z_).start())

        @pl.when(has_extra > 0)
        def _():
            v[r, core, x, NZ + which] = value[TILE:]
            over_z(lambda z_: gz_extra(v, r, q, which, z_).start())

        def drain():
            over_z(lambda z_: gz_main(v, r, q, z, z_).wait_send())

            @pl.when(has_extra > 0)
            def _():
                over_z(lambda z_: gz_extra(v, r, q, which, z_).wait_send())
        drains.append(drain)

    def gather_z_wait(v, r, q):
        over_z(lambda z_: gz_main(v, r, q, z_, z_).wait_recv())
        for e in range(extras):
            @pl.when(z != extra_owner(e, core))
            def _():
                gz_extra(v, r, q, e, extra_owner(e, core)).wait_recv()

    def g_core(v, r, q, c_, p):
        ref = v.at[r, c_, p]
        return push(ref, ref, ac_s.at[q, p], ac_r.at[q, p], sibling)

    def g_x(v, r, q, p, dest):
        ref = v.at[r, core, p]
        return push(ref, ref, ax_s.at[q, dest], ax_r.at[q, p], at(dest, z, core))

    def gather_x_start(v, r, q):
        for d in hops4:
            go(g_x(v, r, q, x, x_peer(d)))
        go(g_core(v, r, q, core, x))

    def gather_x_forward(v, r, q):
        for d in (1, 3, 2):
            p = x_peer(d)
            g_x(v, r, q, p, p).wait_recv()
            go(g_core(v, r, q, core, p))

    def gather_core_wait(v, r, q):
        for d in (0, 1, 3, 2):
            g_core(v, r, q, 1 - core, wrap(x + d, NX)).wait_recv()

    def forward(r):
        value = vh[r].reshape(columns, 128)
        return jnp.dot(d_ref[...], value, preferred_element_type=F32) * mask_ref[...]

    def y_start(r, partial, norms):
        yb[r, y] = partial
        ny[r, y] = norms
        for d in hops4:
            y_ = wrap(y + d, NY)
            go(push(ny.at[r, y], ny.at[r, y], ny_s.at[r, y_], ny_r.at[r, y], y_peer(d)))
            go(push(yb.at[r, y], yb.at[r, y], y_s.at[r, y_], y_r.at[r, y], y_peer(d)))

    def y_wait(r):
        for d in hops4:
            y_ = wrap(y + d, NY)
            push(ny.at[r, y], ny.at[r, y_], ny_s.at[r, y_], ny_r.at[r, y_], y_peer(d)).wait_recv()
            push(yb.at[r, y], yb.at[r, y_], y_s.at[r, y_], y_r.at[r, y_], y_peer(d)).wait_recv()
        return (
            (yb[r, 0] + yb[r, 1]) + (yb[r, 2] + yb[r, 3]),
            (ny[r, 0] + ny[r, 1]) + (ny[r, 2] + ny[r, 3]),
        )

    def split(value):
        hi = value.astype(BF16)
        return hi, (value - hi.astype(F32)).astype(BF16)

    def gather(r, k, value, norms):
        hi, lo = split(value)
        gather_z_start(vh, r, 2 * r, hi)
        n_z(k, norms)
        gather_z_start(vl, r, 2 * r + 1, lo)
        gather_z_wait(vh, r, 2 * r)
        gather_x_start(vh, r, 2 * r)
        n_x(k, n_z_sum(k))
        gather_x_forward(vh, r, 2 * r)
        n_core(k, n_x_sum(k))
        gather_core_wait(vh, r, 2 * r)
        return n_core_sum(k)

    def root(v):
        return jnp.sqrt(v + EPS)

    def walk_of(v):
        return w_own * (turn(v) - v)

    got, norm = reduce_scatter(0, 0, padded([total(bc * bc)]))
    beta1 = root(fold(norm[0:1]))
    v1 = got / beta1
    dv = walk_of(v1)
    dv8 = dv * 0.125
    norms = gather(0, 1, v1, padded([total(v1 * v1), total(dv8 * dv8)]))
    y_start(0, compact(forward(0)), norms)
    gather_z_wait(vl, 0, 1)
    gather_x_start(vl, 0, 1)
    image, norms = y_wait(0)

    alpha1 = root(fold(norms[0:1]))
    o2 = image / alpha1 - alpha1 * (bc_ref[...] / beta1)
    u_ref[1] = expand(o2)
    walk2 = (norms[1:2] / (alpha1 * alpha1)) * 64.0
    got, norm = reduce_scatter(1, 2, padded([total(o2 * o2)]))
    beta2 = jnp.sqrt(fold(norm[0:1]) + walk2 + EPS)
    wz = (dv / alpha1) / beta2
    v2 = got / beta2 - w_own * wz - beta2 * (v1 / alpha1)
    dv8 = walk_of(v2) * 0.125
    norms = gather(
        1, 3, v2,
        padded([total(v2 * v2), total(dv8 * dv8), total(dv8 * wz), total(wz * wz)]),
    )
    y_start(1, compact(forward(1)), norms)
    gather_z_wait(vl, 1, 3)
    gather_x_start(vl, 1, 3)
    gather_x_forward(vl, 0, 1)
    image, norms = y_wait(1)

    alpha2 = root(fold(norms[0:1]))
    o3 = image / alpha2 - alpha2 * (o2 / beta2)
    n_core(4, padded([total(o3 * o3)]))
    square = alpha2 * alpha2
    walk3 = (norms[1:2] / square) * 64.0 - 16.0 * norms[2:3] + square * norms[3:4]
    walk3 = jnp.maximum(walk3, 0.0)
    n_x(4, n_core_sum(4))
    gather_x_forward(vl, 1, 3)
    n_z(4, n_x_sum(4))
    rho1 = jnp.sqrt(alpha1 * alpha1 + beta2 * beta2)
    cos1, sin1 = alpha1 / rho1, beta2 / rho1
    first_step = cos1 * beta1 / rho1
    phi_bar = sin1 * beta1
    rho_bar = -cos1 * alpha2
    theta = sin1 * alpha2 / rho1
    gather_core_wait(vl, 0, 1)
    gather_core_wait(vl, 1, 3)
    beta3 = jnp.sqrt(fold(n_z_sum(4)[0:1]) + walk3 + EPS)
    rho2 = jnp.sqrt(rho_bar * rho_bar + beta3 * beta3)
    second_step = (rho_bar / rho2) * phi_bar / rho2
    weight1 = (first_step - second_step * theta) / alpha1
    weight2 = second_step / alpha2
    for c_ in range(NC):
        for p in range(NX):
            first = (vh[0, c_, p].astype(F32) + vl[0, c_, p].astype(F32)).reshape(piece, 128)
            second = (vh[1, c_, p].astype(F32) + vl[1, c_, p].astype(F32)).reshape(piece, 128)
            begin = (c_ * NX + p) * piece
            out[begin:begin + piece, :] = weight1 * first + weight2 * second

    for drain in drains:
        drain()


def body(design, observed, arc_lengths, arc_months, walk_weight):
    rows, columns = design.shape
    tiles = columns // (NC * NX * TILE)
    vmem = pl.BlockSpec(memory_space=pltpu.VMEM)
    smem = pl.BlockSpec(memory_space=pltpu.SMEM)
    dma = pltpu.SemaphoreType.DMA
    block = (tiles, TILE, 128)
    scratch = [
        pltpu.VMEM((rows, columns), BF16),
        pltpu.VMEM((columns, rows), BF16),
        pltpu.VMEM((2, 128, 128), F32),
        pltpu.VMEM((rows, 128), F32),
        pltpu.VMEM((2, rows, 128), BF16),
        pltpu.VMEM((rows // 2, 128), F32),
        pltpu.VMEM((2, NX) + block, F32),
        pltpu.VMEM((2, NX) + block, F32),
        pltpu.VMEM((2, NX) + block, F32),
        pltpu.VMEM((2, NX) + block, F32),
        pltpu.VMEM((2,) + block, F32),
        pltpu.VMEM((2, 2, NZ, TILE, 128), F32),
        pltpu.VMEM((2, 2, TILE, 128), F32),
        pltpu.VMEM((2, NC, NX) + block, BF16),
        pltpu.VMEM((2, NC, NX) + block, BF16),
        pltpu.VMEM((2, NY, rows // 2, 128), F32),
        pltpu.VMEM((2, NY, 4, 128), F32),
        pltpu.VMEM((5, NC, 4, 128), F32),
        pltpu.VMEM((5, NX, 4, 128), F32),
        pltpu.VMEM((5, NZ, 4, 128), F32),
        dma,
        dma((2, NX)), dma((2, NX)),
        dma((2, NX)), dma((2, NX)),
        dma((2, 2, NZ)), dma((2, 2, NZ)),
        dma((4, 2, NZ)), dma((4, 2, NZ)),
        dma((4, NX)), dma((4, NX)),
        dma((4, NX)), dma((4, NX)),
        dma((2, NY)), dma((2, NY)),
        dma((2, NY)), dma((2, NY)),
        dma((5,)), dma((5,)),
        dma((5, NX)), dma((5, NX)),
        dma((5, NZ)), dma((5, NZ)),
    ]
    return pl.pallas_call(
        kernel,
        out_shape=jax.ShapeDtypeStruct((columns, 128), F32),
        in_specs=[pl.BlockSpec(memory_space=pl.ANY), vmem, smem, smem, vmem],
        out_specs=vmem,
        scratch_shapes=scratch,
        compiler_params=pltpu.CompilerParams(
            collective_id=0, has_side_effects=True, vmem_limit_bytes=40 * 1024 * 1024
        ),
    )(design, observed, arc_lengths, arc_months, walk_weight.reshape(1, columns))


def solution(mesh):
    in_specs = (P("arcs", "coef"), P("arcs", None), P("arcs", None), P("arcs", None), P("coef"))
    return jax.shard_map(
        body, mesh=mesh, in_specs=in_specs, out_specs=P("coef", None), check_vma=False
    )
```

```python
import functools

import jax
import jax.numpy as jnp
from jax import lax
from jax.experimental import pallas as pl
from jax.experimental.pallas import tpu as pltpu
from jax.sharding import PartitionSpec as P

NCOEF = 9405
EPS = 1e-06
MESH = pl.DeviceIdType.MESH
NX, NZ, NC, NY = 4, 16, 2, 4
TILE = 16
F32, BF16 = jnp.float32, jnp.bfloat16


def kernel(
    design, observed, lengths, months, walk, out,
    d_ref, dt, ob_ref, len_ref, mon_ref, walk_ref, wt, mask_ref, u_ref, bc_ref,
    cs, cr, xs, xr, tb, zr, own, vh, vl, yb, ny, nc, nx, nz,
    in_sem, cs_s, cs_r, xs_s, xs_r, zs_s, zs_r,
    az_s, az_r, ax_s, ax_r, ac_s, ac_r, y_s, y_r, ny_s, ny_r,
    nc_s, nc_r, nx_s, nx_r, nz_s, nz_r,
):
    rows = d_ref.shape[0]
    columns = d_ref.shape[1]
    tiles = columns // (NC * NX * TILE)
    piece = tiles * TILE
    extras = tiles - NZ
    arc, y = lax.axis_index("arcs"), lax.axis_index("coef")
    core = lax.rem(arc, NC)
    z = lax.rem(arc // NC, NZ)
    x = arc // (NC * NZ)

    def at(x_, z_, c_):
        return ((x_ * NZ + z_) * NC + c_, y)

    def wrap(v, n):
        return lax.rem(v, n)

    sibling = at(x, z, 1 - core)
    hops4 = (2, 1, 3)

    def x_peer(d):
        return wrap(x + d, NX)

    def y_peer(d):
        return (arc, wrap(y + d, NY))

    def extra_owner(e, c_):
        return 5 * e + 3 * c_

    drains = []

    def push(src, dst, ssem, rsem, dev):
        return pltpu.make_async_remote_copy(
            src_ref=src, dst_ref=dst, send_sem=ssem, recv_sem=rsem,
            device_id=dev, device_id_type=MESH,
        )

    def go(copy):
        copy.start()
        drains.append(copy.wait_send)

    def over_z(body):
        def step(i, _):
            away = lax.div(i + 1, 2) * (1 - 2 * lax.rem(i, 2))
            body(wrap(z + NZ // 2 + away, NZ))
            return 0
        lax.fori_loop(0, NZ - 1, step, 0)

    barrier = pltpu.get_barrier_semaphore()

    def greet(dev):
        pl.semaphore_signal(barrier, inc=1, device_id=dev, device_id_type=MESH)

    over_z(lambda z_: greet(at(x, z_, core)))
    for d in hops4:
        greet(at(x_peer(d), z, core))
        greet(y_peer(d))
    greet(sibling)

    has_extra = jnp.int32(0)
    which = jnp.int32(0)
    for e in range(extras):
        hit = (z == extra_owner(e, core)).astype(jnp.int32)
        has_extra = has_extra + hit
        which = which + e * hit
    base = (core * NX + x) * piece
    firsts = [base + z * TILE, base + (NZ + which) * TILE]

    loads = [
        pltpu.make_async_copy(src, dst, in_sem.at[i])
        for i, (src, dst) in enumerate([
            (lengths, len_ref), (months, mon_ref), (observed, ob_ref), (design, d_ref),
        ] + [
            (walk.at[pl.ds(pl.multiple_of(f // 128 * 128, 128), 128)], walk_ref.at[s])
            for s, f in enumerate(firsts)
        ])
    ]
    for load in loads:
        load.start()

    lane = lax.broadcasted_iota(jnp.int32, (rows, 128), 1)
    row = lax.broadcasted_iota(jnp.int32, (rows, 128), 0)
    start = jnp.int32(0)
    month_row = jnp.full((rows, 128), -1, jnp.int32)
    loads[0].wait()
    loads[1].wait()
    for j in range(len_ref.shape[1]):
        end = start + len_ref[0, j]
        month_row = jnp.where((row >= start) & (row < end), mon_ref[0, j], month_row)
        start = end
    side = (lane >= 64).astype(jnp.int32)
    mask_stack = (month_row == side).astype(F32)
    mask_ref[...] = mask_stack
    half = rows // 2
    low = lax.broadcasted_iota(jnp.int32, (half, 128), 1) < 64
    loads[2].wait()
    ob = ob_ref[...].astype(F32)
    ob = jnp.concatenate([ob, ob], axis=0).T * mask_stack

    def turn(v):
        return pltpu.roll(v, 64, 1)

    def compact(v):
        s = v + turn(v)
        return jnp.where(low, s[:half], s[half:])

    def expand(v):
        t = turn(v)
        first = jnp.where(low, v, t)
        second = jnp.where(low, t, v)
        return (jnp.concatenate([first, second], axis=0) * mask_ref[...]).astype(BF16)

    def fold(v):
        return v + turn(jnp.broadcast_to(v, (8, 128)))[:1]

    def total(v):
        return jnp.sum(v, axis=0, keepdims=True)

    def padded(parts):
        rest = 4 - len(parts)
        if rest:
            parts = parts + [jnp.zeros((rest, 128), F32)]
        return jnp.concatenate(parts, axis=0)

    bc = compact(ob)
    bc_ref[...] = bc
    u_ref[0] = expand(bc)

    row16 = lax.broadcasted_iota(jnp.int32, (TILE, 128), 0)
    w_parts, keep_parts = [], []
    for s in range(2):
        first = firsts[s]
        inside = lax.rem(first, 128)
        loads[4 + s].wait()
        wt[s] = jnp.broadcast_to(walk_ref[s:s + 1, :], (128, 128)).T
        w_parts.append(wt[s, pl.ds(pl.multiple_of(inside, TILE), TILE), :])
        keep = (y * columns + first + row16) < NCOEF
        if s == 1:
            keep = keep & (jnp.full((TILE, 128), has_extra, jnp.int32) > 0)
        keep_parts.append(keep.astype(F32))
    w_own = jnp.concatenate(w_parts, axis=0)
    keep_own = jnp.concatenate(keep_parts, axis=0)

    loads[3].wait()
    for j in range(columns // 128):
        dt[j * 128:(j + 1) * 128, :] = d_ref[:, j * 128:(j + 1) * 128].T
    pl.semaphore_wait(barrier, 1 + 2 * len(hops4) + NZ - 1)

    def n_core(k, value):
        nc[k, core] = value
        go(push(nc.at[k, core], nc.at[k, core], nc_s.at[k], nc_r.at[k], sibling))

    def n_core_sum(k):
        push(nc.at[k, core], nc.at[k, 1 - core], nc_s.at[k], nc_r.at[k], sibling).wait_recv()
        return nc[k, 0] + nc[k, 1]

    def n_x(k, value):
        nx[k, x] = value
        for d in hops4:
            x_ = x_peer(d)
            go(push(nx.at[k, x], nx.at[k, x], nx_s.at[k, x_], nx_r.at[k, x], at(x_, z, core)))

    def n_x_sum(k):
        for d in hops4:
            x_ = x_peer(d)
            push(nx.at[k, x], nx.at[k, x_], nx_s.at[k, x_], nx_r.at[k, x_], at(x_, z, core)).wait_recv()
        return (nx[k, 0] + nx[k, 1]) + (nx[k, 2] + nx[k, 3])

    def n_z_copy(k, z_):
        return push(nz.at[k, z], nz.at[k, z], nz_s.at[k, z_], nz_r.at[k, z], at(x, z_, core))

    def n_z(k, value):
        nz[k, z] = value
        over_z(lambda z_: n_z_copy(k, z_).start())
        drains.append(lambda: over_z(lambda z_: n_z_copy(k, z_).wait_send()))

    def n_z_sum(k):
        over_z(lambda z_: push(
            nz.at[k, z], nz.at[k, z_], nz_s.at[k, z_], nz_r.at[k, z_], at(x, z_, core)).wait_recv())
        return jnp.sum(nz[k], axis=0)

    def adjoint_piece(r, h, p):
        first = pl.multiple_of((h * NX + p) * piece, TILE)
        value = jnp.dot(dt[pl.ds(first, piece), :], u_ref[r], preferred_element_type=F32)
        return value.reshape(tiles, TILE, 128)

    def reduce_scatter(r, k, norm_value):
        n_core(k, norm_value)
        order = [x_peer(d) for d in hops4] + [x]

        def core_copy(p):
            return push(cs.at[r, p], cr.at[r, p], cs_s.at[r, p], cs_r.at[r, p], sibling)

        for p in order:
            cs[r, p] = adjoint_piece(r, 1 - core, p)
            go(core_copy(p))
        for i, p in enumerate(order):
            mine = adjoint_piece(r, core, p)
            core_copy(p).wait_recv()
            mine = mine + cr[r, p]
            if i < 3:
                xs[r, p] = mine
                go(push(xs.at[r, p], xr.at[r, x], xs_s.at[r, p], xs_r.at[r, x], at(p, z, core)))
            else:
                xr[r, x] = mine
            if i == 0:
                n_x(k, n_core_sum(k))
        n_z(k, n_x_sum(k))
        for p in order[:3]:
            push(xs.at[r, p], xr.at[r, p], xs_s.at[r, p], xs_r.at[r, p], at(p, z, core)).wait_recv()
        tb[r] = (xr[r, 0] + xr[r, 1]) + (xr[r, 2] + xr[r, 3])

        def main_copy(z_, src):
            return push(tb.at[r, z_], zr.at[r, 0, src], zs_s.at[r, 0, z_], zs_r.at[r, 0, src], at(x, z_, core))

        def extra_copy(e, src):
            z_ = extra_owner(e, core)
            return push(tb.at[r, NZ + e], zr.at[r, 1, src], zs_s.at[r, 1, z_], zs_r.at[r, 1, src], at(x, z_, core))

        for e in range(extras):
            @pl.when(z != extra_owner(e, core))
            def _():
                extra_copy(e, z).start()
        over_z(lambda z_: main_copy(z_, z).start())
        zr[r, 0, z] = tb[r, z]
        over_z(lambda z_: main_copy(z_, z_).wait_recv())
        own[r, 0] = jnp.sum(zr[r, 0], axis=0)
        own[r, 1] = jnp.zeros((TILE, 128), F32)

        @pl.when(has_extra > 0)
        def _():
            zr[r, 1, z] = tb[r, NZ + which]
            over_z(lambda z_: push(
                tb.at[r, NZ], zr.at[r, 1, z_], zs_s.at[r, 1, z_], zs_r.at[r, 1, z_], at(x, z_, core)).wait_recv())
            own[r, 1] = jnp.sum(zr[r, 1], axis=0)

        def drain():
            over_z(lambda z_: main_copy(z_, z).wait_send())
            for e in range(extras):
                @pl.when(z != extra_owner(e, core))
                def _():
                    extra_copy(e, z).wait_send()
        drains.append(drain)
        norm = n_z_sum(k)
        return own[r].reshape(2 * TILE, 128) * keep_own, norm

    def gz_main(v, r, q, src, z_):
        ref = v.at[r, core, x, src]
        return push(ref, ref, az_s.at[q, 0, z_], az_r.at[q, 0, src], at(x, z_, core))

    def gz_extra(v, r, q, e, z_):
        ref = v.at[r, core, x, NZ + e]
        return push(ref, ref, az_s.at[q, 1, z_], az_r.at[q, 1, e], at(x, z_, core))

    def gather_z_start(v, r, q, value):
        v[r, core, x, z] = value[:TILE]
        over_z(lambda z_: gz_main(v, r, q, z, z_).start())

        @pl.when(has_extra > 0)
        def _():
            v[r, core, x, NZ + which] = value[TILE:]
            over_z(lambda z_: gz_extra(v, r, q, which, z_).start())

        def drain():
            over_z(lambda z_: gz_main(v, r, q, z, z_).wait_send())

            @pl.when(has_extra > 0)
            def _():
                over_z(lambda z_: gz_extra(v, r, q, which, z_).wait_send())
        drains.append(drain)

    def gather_z_wait(v, r, q):
        over_z(lambda z_: gz_main(v, r, q, z_, z_).wait_recv())
        for e in range(extras):
            @pl.when(z != extra_owner(e, core))
            def _():
                gz_extra(v, r, q, e, extra_owner(e, core)).wait_recv()

    def g_core(v, r, q, c_, p):
        ref = v.at[r, c_, p]
        return push(ref, ref, ac_s.at[q, p], ac_r.at[q, p], sibling)

    def g_x(v, r, q, p, dest):
        ref = v.at[r, core, p]
        return push(ref, ref, ax_s.at[q, dest], ax_r.at[q, p], at(dest, z, core))

    def gather_x_start(v, r, q):
        for d in hops4:
            go(g_x(v, r, q, x, x_peer(d)))
        go(g_core(v, r, q, core, x))

    def gather_x_forward(v, r, q):
        for d in (1, 3, 2):
            p = x_peer(d)
            g_x(v, r, q, p, p).wait_recv()
            go(g_core(v, r, q, core, p))

    def gather_core_wait(v, r, q):
        for d in (0, 1, 3, 2):
            g_core(v, r, q, 1 - core, wrap(x + d, NX)).wait_recv()

    def forward(r):
        value = vh[r].reshape(columns, 128)
        return jnp.dot(d_ref[...], value, preferred_element_type=F32) * mask_ref[...]

    def y_start(r, partial, norms):
        yb[r, y] = partial
        ny[r, y] = norms
        for d in hops4:
            y_ = wrap(y + d, NY)
            go(push(ny.at[r, y], ny.at[r, y], ny_s.at[r, y_], ny_r.at[r, y], y_peer(d)))
            go(push(yb.at[r, y], yb.at[r, y], y_s.at[r, y_], y_r.at[r, y], y_peer(d)))

    def y_wait(r):
        for d in hops4:
            y_ = wrap(y + d, NY)
            push(ny.at[r, y], ny.at[r, y_], ny_s.at[r, y_], ny_r.at[r, y_], y_peer(d)).wait_recv()
            push(yb.at[r, y], yb.at[r, y_], y_s.at[r, y_], y_r.at[r, y_], y_peer(d)).wait_recv()
        return (
            (yb[r, 0] + yb[r, 1]) + (yb[r, 2] + yb[r, 3]),
            (ny[r, 0] + ny[r, 1]) + (ny[r, 2] + ny[r, 3]),
        )

    def split(value):
        hi = value.astype(BF16)
        return hi, (value - hi.astype(F32)).astype(BF16)

    def gather(r, k, value, norms):
        hi, lo = split(value)
        gather_z_start(vh, r, 2 * r, hi)
        n_z(k, norms)
        gather_z_start(vl, r, 2 * r + 1, lo)
        gather_z_wait(vh, r, 2 * r)
        gather_x_start(vh, r, 2 * r)
        n_x(k, n_z_sum(k))
        gather_x_forward(vh, r, 2 * r)
        n_core(k, n_x_sum(k))
        gather_core_wait(vh, r, 2 * r)
        return n_core_sum(k)

    def root(v):
        return jnp.sqrt(v + EPS)

    def walk_of(v):
        return w_own * (turn(v) - v)

    got, norm = reduce_scatter(0, 0, padded([total(bc * bc)]))
    beta1 = root(fold(norm[0:1]))
    v1 = got / beta1
    dv = walk_of(v1)
    dv8 = dv * 0.125
    norms = gather(0, 1, v1, padded([total(v1 * v1), total(dv8 * dv8)]))
    y_start(0, compact(forward(0)), norms)
    gather_z_wait(vl, 0, 1)
    gather_x_start(vl, 0, 1)
    image, norms = y_wait(0)

    alpha1 = root(fold(norms[0:1]))
    o2 = image / alpha1 - alpha1 * (bc_ref[...] / beta1)
    u_ref[1] = expand(o2)
    walk2 = (norms[1:2] / (alpha1 * alpha1)) * 64.0
    got, norm = reduce_scatter(1, 2, padded([total(o2 * o2)]))
    beta2 = jnp.sqrt(fold(norm[0:1]) + walk2 + EPS)
    wz = (dv / alpha1) / beta2
    v2 = got / beta2 - w_own * wz - beta2 * (v1 / alpha1)
    dv8 = walk_of(v2) * 0.125
    norms = gather(
        1, 3, v2,
        padded([total(v2 * v2), total(dv8 * dv8), total(dv8 * wz), total(wz * wz)]),
    )
    y_start(1, compact(forward(1)), norms)
    gather_z_wait(vl, 1, 3)
    gather_x_start(vl, 1, 3)
    gather_x_forward(vl, 0, 1)
    image, norms = y_wait(1)

    alpha2 = root(fold(norms[0:1]))
    o3 = image / alpha2 - alpha2 * (o2 / beta2)
    n_core(4, padded([total(o3 * o3)]))
    square = alpha2 * alpha2
    walk3 = (norms[1:2] / square) * 64.0 - 16.0 * norms[2:3] + square * norms[3:4]
    walk3 = jnp.maximum(walk3, 0.0)
    n_x(4, n_core_sum(4))
    gather_x_forward(vl, 1, 3)
    n_z(4, n_x_sum(4))
    rho1 = jnp.sqrt(alpha1 * alpha1 + beta2 * beta2)
    cos1, sin1 = alpha1 / rho1, beta2 / rho1
    first_step = cos1 * beta1 / rho1
    phi_bar = sin1 * beta1
    rho_bar = -cos1 * alpha2
    theta = sin1 * alpha2 / rho1
    gather_core_wait(vl, 0, 1)
    gather_core_wait(vl, 1, 3)
    beta3 = jnp.sqrt(fold(n_z_sum(4)[0:1]) + walk3 + EPS)
    rho2 = jnp.sqrt(rho_bar * rho_bar + beta3 * beta3)
    second_step = (rho_bar / rho2) * phi_bar / rho2
    weight1 = (first_step - second_step * theta) / alpha1
    weight2 = second_step / alpha2
    for c_ in range(NC):
        for p in range(NX):
            first = (vh[0, c_, p].astype(F32) + vl[0, c_, p].astype(F32)).reshape(piece, 128)
            second = (vh[1, c_, p].astype(F32) + vl[1, c_, p].astype(F32)).reshape(piece, 128)
            begin = (c_ * NX + p) * piece
            out[begin:begin + piece, :] = weight1 * first + weight2 * second

    for drain in drains:
        drain()


def body(design, observed, arc_lengths, arc_months, walk_weight):
    rows, columns = design.shape
    tiles = columns // (NC * NX * TILE)
    vmem = pl.BlockSpec(memory_space=pltpu.VMEM)
    hbm = pl.BlockSpec(memory_space=pltpu.HBM)
    dma = pltpu.SemaphoreType.DMA
    block = (tiles, TILE, 128)
    scratch = [
        pltpu.VMEM((rows, columns), BF16),
        pltpu.VMEM((columns, rows), BF16),
        pltpu.VMEM((observed.shape[1], rows), BF16),
        pltpu.SMEM(arc_lengths.shape, jnp.int32),
        pltpu.SMEM(arc_months.shape, jnp.int32),
        pltpu.VMEM((2, 128), F32),
        pltpu.VMEM((2, 128, 128), F32),
        pltpu.VMEM((rows, 128), F32),
        pltpu.VMEM((2, rows, 128), BF16),
        pltpu.VMEM((rows // 2, 128), F32),
        pltpu.VMEM((2, NX) + block, F32),
        pltpu.VMEM((2, NX) + block, F32),
        pltpu.VMEM((2, NX) + block, F32),
        pltpu.VMEM((2, NX) + block, F32),
        pltpu.VMEM((2,) + block, F32),
        pltpu.VMEM((2, 2, NZ, TILE, 128), F32),
        pltpu.VMEM((2, 2, TILE, 128), F32),
        pltpu.VMEM((2, NC, NX) + block, BF16),
        pltpu.VMEM((2, NC, NX) + block, BF16),
        pltpu.VMEM((2, NY, rows // 2, 128), F32),
        pltpu.VMEM((2, NY, 4, 128), F32),
        pltpu.VMEM((5, NC, 4, 128), F32),
        pltpu.VMEM((5, NX, 4, 128), F32),
        pltpu.VMEM((5, NZ, 4, 128), F32),
        dma((6,)),
        dma((2, NX)), dma((2, NX)),
        dma((2, NX)), dma((2, NX)),
        dma((2, 2, NZ)), dma((2, 2, NZ)),
        dma((4, 2, NZ)), dma((4, 2, NZ)),
        dma((4, NX)), dma((4, NX)),
        dma((4, NX)), dma((4, NX)),
        dma((2, NY)), dma((2, NY)),
        dma((2, NY)), dma((2, NY)),
        dma((5,)), dma((5,)),
        dma((5, NX)), dma((5, NX)),
        dma((5, NZ)), dma((5, NZ)),
    ]
    return pl.pallas_call(
        kernel,
        out_shape=jax.ShapeDtypeStruct((columns, 128), F32),
        in_specs=[hbm] * 5,
        out_specs=vmem,
        scratch_shapes=scratch,
        compiler_params=pltpu.CompilerParams(
            collective_id=0, has_side_effects=True, vmem_limit_bytes=63 * 1024 * 1024
        ),
    )(design, observed.T, arc_lengths, arc_months, walk_weight)


def solution(mesh):
    in_specs = (P("arcs", "coef"), P("arcs", None), P("arcs", None), P("arcs", None), P("coef"))
    return jax.shard_map(
        body, mesh=mesh, in_specs=in_specs, out_specs=P("coef", None), check_vma=False
    )
```

```python
import functools

import jax
import jax.numpy as jnp
from jax import lax
from jax.experimental import pallas as pl
from jax.experimental.pallas import tpu as pltpu
from jax.sharding import PartitionSpec as P

NCOEF = 9405
EPS = 1e-06
MESH = pl.DeviceIdType.MESH
NX, NZ, NC, NY = 4, 16, 2, 4
TILE = 16
F32, BF16 = jnp.float32, jnp.bfloat16


def kernel(
    design, observed, lengths, months, walk, out,
    d_ref, dt, ob_ref, len_ref, mon_ref, walk_ref, wt, mask_ref, u_ref, bc_ref,
    cs, cr, xs, xr, tb, zr, own, vh, vl, yb, nc, nx, nz,
    in_sem, cs_s, cs_r, xs_s, xs_r, zs_s, zs_r, ze_s, ze_r,
    az_s, az_r, ae_s, ae_r, ax_s, ax_r, ac_s, ac_r, y_s, y_r,
    nc_s, nc_r, nx_s, nx_r, nz_s, nz_r,
):
    rows = d_ref.shape[0]
    columns = d_ref.shape[1]
    tiles = columns // (NC * NX * TILE)
    piece = tiles * TILE
    extras = tiles - NZ
    arc, y = lax.axis_index("arcs"), lax.axis_index("coef")
    core = lax.rem(arc, NC)
    z = lax.rem(arc // NC, NZ)
    x = arc // (NC * NZ)

    def at(x_, z_, c_):
        return ((x_ * NZ + z_) * NC + c_, y)

    def wrap(v, n):
        return lax.rem(v, n)

    sibling = at(x, z, 1 - core)
    hops4 = (2, 1, 3)

    def x_peer(d):
        return wrap(x + d, NX)

    def y_peer(d):
        return (arc, wrap(y + d, NY))

    def extra_owner(e, c_):
        return 5 * e + 3 * c_

    drains = []

    def push(src, dst, ssem, rsem, dev):
        return pltpu.make_async_remote_copy(
            src_ref=src, dst_ref=dst, send_sem=ssem, recv_sem=rsem,
            device_id=dev, device_id_type=MESH,
        )

    def sent(ref, sem):
        drains.append(push(ref, ref, sem, sem, sibling).wait_send)

    def received(ref, sem):
        push(ref, ref, sem, sem, sibling).wait_recv()

    def nth(i, middle):
        return middle + lax.div(i + 1, 2) * (1 - 2 * lax.rem(i, 2))

    def loop(count, body):
        def step(i, _):
            body(i)
            return 0
        lax.fori_loop(0, count, step, 0)

    def over_z(body):
        loop(NZ - 1, lambda i: body(wrap(z + nth(i, NZ // 2), NZ)))

    def over_x(body):
        loop(NX - 1, lambda i: body(wrap(x + nth(i, NX // 2), NX)))

    barrier = pltpu.get_barrier_semaphore()

    def greet(dev):
        pl.semaphore_signal(barrier, inc=1, device_id=dev, device_id_type=MESH)

    over_z(lambda z_: greet(at(x, z_, core)))
    for d in hops4:
        greet(at(x_peer(d), z, core))
        greet(y_peer(d))
    greet(sibling)

    has_extra = jnp.int32(0)
    which = jnp.int32(0)
    for e in range(extras):
        hit = (z == extra_owner(e, core)).astype(jnp.int32)
        has_extra = has_extra + hit
        which = which + e * hit
    base = (core * NX + x) * piece
    firsts = [base + z * TILE, base + (NZ + which) * TILE]

    loads = [
        pltpu.make_async_copy(src, dst, in_sem.at[i])
        for i, (src, dst) in enumerate([
            (lengths, len_ref), (months, mon_ref), (observed, ob_ref), (design, d_ref),
        ] + [
            (walk.at[pl.ds(pl.multiple_of(f // 128 * 128, 128), 128)], walk_ref.at[s])
            for s, f in enumerate(firsts)
        ])
    ]
    for load in loads:
        load.start()

    lane = lax.broadcasted_iota(jnp.int32, (rows, 128), 1)
    row = lax.broadcasted_iota(jnp.int32, (rows, 128), 0)
    start = jnp.int32(0)
    month_row = jnp.full((rows, 128), -1, jnp.int32)
    loads[0].wait()
    loads[1].wait()
    for j in range(len_ref.shape[1]):
        end = start + len_ref[0, j]
        month_row = jnp.where((row >= start) & (row < end), mon_ref[0, j], month_row)
        start = end
    side = (lane >= 64).astype(jnp.int32)
    mask_stack = (month_row == side).astype(F32)
    mask_ref[...] = mask_stack
    half = rows // 2
    low = lax.broadcasted_iota(jnp.int32, (half, 128), 1) < 64
    loads[2].wait()
    ob = ob_ref[...].astype(F32)
    ob = jnp.concatenate([ob, ob], axis=0).T * mask_stack

    def turn(v):
        return pltpu.roll(v, 64, 1)

    def compact(v):
        s = v + turn(v)
        return jnp.where(low, s[:half], s[half:])

    def expand(v):
        t = turn(v)
        first = jnp.where(low, v, t)
        second = jnp.where(low, t, v)
        return (jnp.concatenate([first, second], axis=0) * mask_ref[...]).astype(BF16)

    def fold(v):
        return v + turn(jnp.broadcast_to(v, (8, 128)))[:1]

    def total(v):
        return jnp.sum(v, axis=0, keepdims=True)

    def padded(parts):
        rest = 4 - len(parts)
        if rest:
            parts = parts + [jnp.zeros((rest, 128), F32)]
        return jnp.concatenate(parts, axis=0)

    bc = compact(ob)
    bc_ref[...] = bc
    u_ref[0] = expand(bc)

    row16 = lax.broadcasted_iota(jnp.int32, (TILE, 128), 0)
    w_parts, keep_parts = [], []
    for s in range(2):
        first = firsts[s]
        inside = lax.rem(first, 128)
        loads[4 + s].wait()
        wt[s] = jnp.broadcast_to(walk_ref[s:s + 1, :], (128, 128)).T
        w_parts.append(wt[s, pl.ds(pl.multiple_of(inside, TILE), TILE), :])
        keep = (y * columns + first + row16) < NCOEF
        if s == 1:
            keep = keep & (jnp.full((TILE, 128), has_extra, jnp.int32) > 0)
        keep_parts.append(keep.astype(F32))
    w_own = jnp.concatenate(w_parts, axis=0)
    keep_own = jnp.concatenate(keep_parts, axis=0)

    loads[3].wait()
    for j in range(columns // 128):
        dt[j * 128:(j + 1) * 128, :] = d_ref[:, j * 128:(j + 1) * 128].T
    pl.semaphore_wait(barrier, 1 + 2 * len(hops4) + NZ - 1)

    def n_core(k, value):
        nc[k, core] = value
        push(nc.at[k, core], nc.at[k, core], nc_s.at[k], nc_r.at[k], sibling).start()
        sent(nc.at[k, 0], nc_s.at[k])

    def n_core_sum(k):
        received(nc.at[k, 0], nc_r.at[k])
        return nc[k, 0] + nc[k, 1]

    def n_x(k, value):
        nx[k, x] = value
        over_x(lambda x_: push(nx.at[k, x], nx.at[k, x], nx_s.at[k], nx_r.at[k], at(x_, z, core)).start())
        sent(nx.at[k, pl.ds(0, NX - 1)], nx_s.at[k])

    def n_x_sum(k):
        received(nx.at[k, pl.ds(0, NX - 1)], nx_r.at[k])
        return (nx[k, 0] + nx[k, 1]) + (nx[k, 2] + nx[k, 3])

    def n_z(k, value):
        nz[k, z] = value
        over_z(lambda z_: push(nz.at[k, z], nz.at[k, z], nz_s.at[k], nz_r.at[k], at(x, z_, core)).start())
        sent(nz.at[k, pl.ds(0, NZ - 1)], nz_s.at[k])

    def n_z_sum(k):
        received(nz.at[k, pl.ds(0, NZ - 1)], nz_r.at[k])
        return jnp.sum(nz[k], axis=0)

    def adjoint_piece(r, h, p):
        first = pl.multiple_of((h * NX + p) * piece, TILE)
        value = jnp.dot(dt[pl.ds(first, piece), :], u_ref[r], preferred_element_type=F32)
        return value.reshape(tiles, TILE, 128)

    def reduce_scatter(r, k, norm_value):
        n_core(k, norm_value)

        def theirs(i):
            p = wrap(x + nth(i, NX // 2), NX)
            cs[r, p] = adjoint_piece(r, 1 - core, p)
            push(cs.at[r, p], cr.at[r, p], cs_s.at[r], cs_r.at[r, p], sibling).start()
        loop(NX, theirs)
        sent(cs.at[r], cs_s.at[r])

        def mine(p):
            value = adjoint_piece(r, core, p)
            received(cr.at[r, p], cs_r.at[r, p])
            return value + cr[r, p]

        def away(p):
            xs[r, p] = mine(p)
            push(xs.at[r, p], xr.at[r, x], xs_s.at[r], xs_r.at[r], at(p, z, core)).start()
        over_x(away)
        sent(xs.at[r, pl.ds(0, NX - 1)], xs_s.at[r])
        n_x(k, n_core_sum(k))
        xr[r, x] = mine(x)
        n_z(k, n_x_sum(k))
        received(xr.at[r, pl.ds(0, NX - 1)], xs_r.at[r])
        tb[r] = (xr[r, 0] + xr[r, 1]) + (xr[r, 2] + xr[r, 3])

        def elsewhere(e, act):
            pl.when(z != extra_owner(e, core))(act)

        for e in range(extras):
            elsewhere(e, lambda e=e: push(
                tb.at[r, NZ + e], zr.at[r, 1, z], ze_s.at[r, e], ze_r.at[r],
                at(x, extra_owner(e, core), core)).start())
        over_z(lambda z_: push(
            tb.at[r, z_], zr.at[r, 0, z], zs_s.at[r], zs_r.at[r], at(x, z_, core)).start())
        sent(tb.at[r, pl.ds(0, NZ - 1)], zs_s.at[r])
        zr[r, 0, z] = tb[r, z]
        own[r, 1] = jnp.zeros((TILE, 128), F32)

        @pl.when(has_extra > 0)
        def _():
            zr[r, 1, z] = tb[r, NZ + which]
            received(zr.at[r, 1, pl.ds(0, NZ - 1)], ze_r.at[r])
            own[r, 1] = jnp.sum(zr[r, 1], axis=0)
        norm = n_z_sum(k)
        received(zr.at[r, 0, pl.ds(0, NZ - 1)], zs_r.at[r])
        own[r, 0] = jnp.sum(zr[r, 0], axis=0)

        def drain():
            for e in range(extras):
                elsewhere(e, lambda e=e: push(
                    tb.at[r, 0], tb.at[r, 0], ze_s.at[r, e], ze_s.at[r, e], sibling).wait_send())
        drains.append(drain)
        return own[r].reshape(2 * TILE, 128) * keep_own, norm

    def gather_z_start(v, r, q, value):
        @pl.when(has_extra > 0)
        def _():
            ref = v.at[r, core, x, NZ + which]
            v[r, core, x, NZ + which] = value[TILE:]
            over_z(lambda z_: push(ref, ref, ae_s.at[q], ae_r.at[q, which], at(x, z_, core)).start())

        main = v.at[r, core, x, z]
        v[r, core, x, z] = value[:TILE]
        over_z(lambda z_: push(main, main, az_s.at[q], az_r.at[q], at(x, z_, core)).start())
        many = v.at[r, core, x, pl.ds(0, NZ - 1)]
        sent(many, az_s.at[q])

        def drain():
            @pl.when(has_extra > 0)
            def _():
                push(many, many, ae_s.at[q], ae_s.at[q], sibling).wait_send()
        drains.append(drain)

    def gather_z_wait(v, r, q):
        received(v.at[r, core, x, pl.ds(0, NZ - 1)], az_r.at[q])
        for e in range(extras):
            @pl.when(z != extra_owner(e, core))
            def _():
                received(v.at[r, core, x, 0], ae_r.at[q, e])

    def to_sibling(v, r, q, p):
        ref = v.at[r, core, p]
        push(ref, ref, ac_s.at[q], ac_r.at[q], sibling).start()

    def gather_x_start(v, r, q):
        ref = v.at[r, core, x]
        over_x(lambda x_: push(ref, ref, ax_s.at[q], ax_r.at[q, x], at(x_, z, core)).start())
        sent(v.at[r, core, pl.ds(0, NX - 1)], ax_s.at[q])
        to_sibling(v, r, q, x)

    def gather_x_forward(v, r, q):
        for d in (1, 3, 2):
            p = x_peer(d)
            received(v.at[r, core, p], ax_r.at[q, p])
            to_sibling(v, r, q, p)
        sent(v.at[r, core], ac_s.at[q])

    def gather_core_wait(v, r, q):
        received(v.at[r, 1 - core], ac_r.at[q])

    def forward(r):
        value = vh[r].reshape(columns, 128)
        return jnp.dot(d_ref[...], value, preferred_element_type=F32) * mask_ref[...]

    def y_start(r, partial, norms):
        yb[r, y, :half] = partial
        yb[r, y, half:half + 8] = jnp.concatenate([norms, jnp.zeros((4, 128), F32)], axis=0)
        for d in hops4:
            push(yb.at[r, y], yb.at[r, y], y_s.at[r], y_r.at[r], y_peer(d)).start()
        sent(yb.at[r, pl.ds(0, NY - 1)], y_s.at[r])

    def y_wait(r):
        received(yb.at[r, pl.ds(0, NY - 1)], y_r.at[r])
        value = (yb[r, 0] + yb[r, 1]) + (yb[r, 2] + yb[r, 3])
        return value[:half], value[half:half + 4]

    def split(value):
        hi = value.astype(BF16)
        return hi, (value - hi.astype(F32)).astype(BF16)

    def gather(r, k, value, norms):
        hi, lo = split(value)
        gather_z_start(vh, r, 2 * r, hi)
        n_z(k, norms)
        gather_z_wait(vh, r, 2 * r)
        gather_x_start(vh, r, 2 * r)
        gather_z_start(vl, r, 2 * r + 1, lo)
        n_x(k, n_z_sum(k))
        gather_x_forward(vh, r, 2 * r)
        n_core(k, n_x_sum(k))
        gather_core_wait(vh, r, 2 * r)
        return n_core_sum(k)

    def root(v):
        return jnp.sqrt(v + EPS)

    def walk_of(v):
        return w_own * (turn(v) - v)

    got, norm = reduce_scatter(0, 0, padded([total(bc * bc)]))
    beta1 = root(fold(norm[0:1]))
    v1 = got / beta1
    dv = walk_of(v1)
    dv8 = dv * 0.125
    norms = gather(0, 1, v1, padded([total(v1 * v1), total(dv8 * dv8)]))
    y_start(0, compact(forward(0)), norms)
    gather_z_wait(vl, 0, 1)
    gather_x_start(vl, 0, 1)
    image, norms = y_wait(0)

    alpha1 = root(fold(norms[0:1]))
    o2 = image / alpha1 - alpha1 * (bc_ref[...] / beta1)
    u_ref[1] = expand(o2)
    walk2 = (norms[1:2] / (alpha1 * alpha1)) * 64.0
    got, norm = reduce_scatter(1, 2, padded([total(o2 * o2)]))
    beta2 = jnp.sqrt(fold(norm[0:1]) + walk2 + EPS)
    wz = (dv / alpha1) / beta2
    v2 = got / beta2 - w_own * wz - beta2 * (v1 / alpha1)
    dv8 = walk_of(v2) * 0.125
    norms = gather(
        1, 3, v2,
        padded([total(v2 * v2), total(dv8 * dv8), total(dv8 * wz), total(wz * wz)]),
    )
    y_start(1, compact(forward(1)), norms)
    gather_z_wait(vl, 1, 3)
    gather_x_start(vl, 1, 3)
    gather_x_forward(vl, 0, 1)
    image, norms = y_wait(1)

    alpha2 = root(fold(norms[0:1]))
    o3 = image / alpha2 - alpha2 * (o2 / beta2)
    n_core(4, padded([total(o3 * o3)]))
    square = alpha2 * alpha2
    walk3 = (norms[1:2] / square) * 64.0 - 16.0 * norms[2:3] + square * norms[3:4]
    walk3 = jnp.maximum(walk3, 0.0)
    n_x(4, n_core_sum(4))
    gather_x_forward(vl, 1, 3)
    n_z(4, n_x_sum(4))
    rho1 = jnp.sqrt(alpha1 * alpha1 + beta2 * beta2)
    cos1, sin1 = alpha1 / rho1, beta2 / rho1
    first_step = cos1 * beta1 / rho1
    phi_bar = sin1 * beta1
    rho_bar = -cos1 * alpha2
    theta = sin1 * alpha2 / rho1
    gather_core_wait(vl, 0, 1)
    gather_core_wait(vl, 1, 3)
    beta3 = jnp.sqrt(fold(n_z_sum(4)[0:1]) + walk3 + EPS)
    rho2 = jnp.sqrt(rho_bar * rho_bar + beta3 * beta3)
    second_step = (rho_bar / rho2) * phi_bar / rho2
    weight1 = (first_step - second_step * theta) / alpha1
    weight2 = second_step / alpha2
    for c_ in range(NC):
        for p in range(NX):
            first = (vh[0, c_, p].astype(F32) + vl[0, c_, p].astype(F32)).reshape(piece, 128)
            second = (vh[1, c_, p].astype(F32) + vl[1, c_, p].astype(F32)).reshape(piece, 128)
            begin = (c_ * NX + p) * piece
            out[begin:begin + piece, :] = weight1 * first + weight2 * second

    for drain in drains:
        drain()


def body(design, observed, arc_lengths, arc_months, walk_weight):
    rows, columns = design.shape
    tiles = columns // (NC * NX * TILE)
    vmem = pl.BlockSpec(memory_space=pltpu.VMEM)
    hbm = pl.BlockSpec(memory_space=pltpu.HBM)
    dma = pltpu.SemaphoreType.DMA
    block = (tiles, TILE, 128)
    scratch = [
        pltpu.VMEM((rows, columns), BF16),
        pltpu.VMEM((columns, rows), BF16),
        pltpu.VMEM((observed.shape[1], rows), BF16),
        pltpu.SMEM(arc_lengths.shape, jnp.int32),
        pltpu.SMEM(arc_months.shape, jnp.int32),
        pltpu.VMEM((2, 128), F32),
        pltpu.VMEM((2, 128, 128), F32),
        pltpu.VMEM((rows, 128), F32),
        pltpu.VMEM((2, rows, 128), BF16),
        pltpu.VMEM((rows // 2, 128), F32),
        pltpu.VMEM((2, NX) + block, F32),
        pltpu.VMEM((2, NX) + block, F32),
        pltpu.VMEM((2, NX) + block, F32),
        pltpu.VMEM((2, NX) + block, F32),
        pltpu.VMEM((2,) + block, F32),
        pltpu.VMEM((2, 2, NZ, TILE, 128), F32),
        pltpu.VMEM((2, 2, TILE, 128), F32),
        pltpu.VMEM((2, NC, NX) + block, BF16),
        pltpu.VMEM((2, NC, NX) + block, BF16),
        pltpu.VMEM((2, NY, rows // 2 + 8, 128), F32),
        pltpu.VMEM((5, NC, 4, 128), F32),
        pltpu.VMEM((5, NX, 4, 128), F32),
        pltpu.VMEM((5, NZ, 4, 128), F32),
        dma((6,)),
        dma((2,)), dma((2, NX)),
        dma((2,)), dma((2,)),
        dma((2,)), dma((2,)),
        dma((2, tiles - NZ)), dma((2,)),
        dma((4,)), dma((4,)),
        dma((4,)), dma((4, tiles - NZ)),
        dma((4,)), dma((4, NX)),
        dma((4,)), dma((4,)),
        dma((2,)), dma((2,)),
        dma((5,)), dma((5,)),
        dma((5,)), dma((5,)),
        dma((5,)), dma((5,)),
    ]
    return pl.pallas_call(
        kernel,
        out_shape=jax.ShapeDtypeStruct((columns, 128), F32),
        in_specs=[hbm] * 5,
        out_specs=vmem,
        scratch_shapes=scratch,
        compiler_params=pltpu.CompilerParams(
            collective_id=0, has_side_effects=True, vmem_limit_bytes=63 * 1024 * 1024
        ),
    )(design, observed.T, arc_lengths, arc_months, walk_weight)


def solution(mesh):
    in_specs = (P("arcs", "coef"), P("arcs", None), P("arcs", None), P("arcs", None), P("coef"))
    return jax.shard_map(
        body, mesh=mesh, in_specs=in_specs, out_specs=P("coef", None), check_vma=False
    )
```

```python
import functools

import jax
import jax.numpy as jnp
from jax import lax
from jax.experimental import pallas as pl
from jax.experimental.pallas import tpu as pltpu
from jax.sharding import PartitionSpec as P

NCOEF = 9405
EPS = 1e-06
MESH = pl.DeviceIdType.MESH
NX, NZ, NC, NY = 4, 16, 2, 4
TILE = 16
SPLIT = 10
F32, BF16 = jnp.float32, jnp.bfloat16


def kernel(
    design, observed, lengths, months, walk, out,
    d_ref, dt, ob_ref, len_ref, mon_ref, walk_ref, wt, mask_ref, u_ref, bc_ref,
    cs, cr, xs, xr, tb, zr, own, vh, vl, yb, nc, nx, nz,
    in_sem, cs_s, cs_r, xs_s, xs_r, zs_s, zs_r, ze_s, ze_r,
    az_s, az_r, ae_s, ae_r, ax_s, ax_r, ac_s, ac_r, y_s, y_r,
    nc_s, nc_r, nx_s, nx_r, nz_s, nz_r,
):
    rows = d_ref.shape[0]
    columns = d_ref.shape[1]
    tiles = columns // (NC * NX * TILE)
    piece = tiles * TILE
    extras = tiles - NZ
    halves = (pl.ds(0, SPLIT), pl.ds(SPLIT, tiles - SPLIT))
    both = pl.ds(0, tiles)
    arc, y = lax.axis_index("arcs"), lax.axis_index("coef")
    core = lax.rem(arc, NC)
    z = lax.rem(arc // NC, NZ)
    x = arc // (NC * NZ)

    def at(x_, z_, c_):
        return ((x_ * NZ + z_) * NC + c_, y)

    def wrap(v, n):
        return lax.rem(v, n)

    sibling = at(x, z, 1 - core)
    hops4 = (2, 1, 3)

    def x_peer(d):
        return wrap(x + d, NX)

    def y_peer(d):
        return (arc, wrap(y + d, NY))

    def extra_owner(e, c_):
        return 3 * e + c_

    drains = []

    def push(src, dst, ssem, rsem, dev):
        return pltpu.make_async_remote_copy(
            src_ref=src, dst_ref=dst, send_sem=ssem, recv_sem=rsem,
            device_id=dev, device_id_type=MESH,
        )

    def sent(ref, sem):
        drains.append(push(ref, ref, sem, sem, sibling).wait_send)

    def received(ref, sem):
        push(ref, ref, sem, sem, sibling).wait_recv()

    def nth(i, middle):
        return middle + lax.div(i + 1, 2) * (1 - 2 * lax.rem(i, 2))

    def loop(count, body):
        def step(i, _):
            body(i)
            return 0
        lax.fori_loop(0, count, step, 0)

    def over_z(body):
        loop(NZ - 1, lambda i: body(wrap(z + nth(i, NZ // 2), NZ)))

    def over_x(body):
        loop(NX - 1, lambda i: body(wrap(x + nth(i, NX // 2), NX)))

    barrier = pltpu.get_barrier_semaphore()

    def greet(dev):
        pl.semaphore_signal(barrier, inc=1, device_id=dev, device_id_type=MESH)

    over_z(lambda z_: greet(at(x, z_, core)))
    for d in hops4:
        greet(at(x_peer(d), z, core))
        greet(y_peer(d))
    greet(sibling)

    has_extra = jnp.int32(0)
    which = jnp.int32(0)
    for e in range(extras):
        hit = (z == extra_owner(e, core)).astype(jnp.int32)
        has_extra = has_extra + hit
        which = which + e * hit
    late = (z >= SPLIT).astype(jnp.int32)
    base = (core * NX + x) * piece
    firsts = [base + z * TILE, base + (NZ + which) * TILE]

    loads = [
        pltpu.make_async_copy(src, dst, in_sem.at[i])
        for i, (src, dst) in enumerate([
            (lengths, len_ref), (months, mon_ref), (observed, ob_ref), (design, d_ref),
        ] + [
            (walk.at[pl.ds(pl.multiple_of(f // 128 * 128, 128), 128)], walk_ref.at[s])
            for s, f in enumerate(firsts)
        ])
    ]
    for load in loads:
        load.start()

    lane = lax.broadcasted_iota(jnp.int32, (rows, 128), 1)
    row = lax.broadcasted_iota(jnp.int32, (rows, 128), 0)
    start = jnp.int32(0)
    month_row = jnp.full((rows, 128), -1, jnp.int32)
    loads[0].wait()
    loads[1].wait()
    for j in range(len_ref.shape[1]):
        end = start + len_ref[0, j]
        month_row = jnp.where((row >= start) & (row < end), mon_ref[0, j], month_row)
        start = end
    side = (lane >= 64).astype(jnp.int32)
    mask_stack = (month_row == side).astype(F32)
    mask_ref[...] = mask_stack
    half = rows // 2
    low = lax.broadcasted_iota(jnp.int32, (half, 128), 1) < 64
    loads[2].wait()
    ob = ob_ref[...].astype(F32)
    ob = jnp.concatenate([ob, ob], axis=0).T * mask_stack

    def turn(v):
        return pltpu.roll(v, 64, 1)

    def compact(v):
        s = v + turn(v)
        return jnp.where(low, s[:half], s[half:])

    def expand(v):
        t = turn(v)
        first = jnp.where(low, v, t)
        second = jnp.where(low, t, v)
        return (jnp.concatenate([first, second], axis=0) * mask_ref[...]).astype(BF16)

    def fold(v):
        return v + turn(jnp.broadcast_to(v, (8, 128)))[:1]

    def total(v):
        return jnp.sum(v, axis=0, keepdims=True)

    def padded(parts):
        rest = 4 - len(parts)
        if rest:
            parts = parts + [jnp.zeros((rest, 128), F32)]
        return jnp.concatenate(parts, axis=0)

    bc = compact(ob)
    bc_ref[...] = bc
    u_ref[0] = expand(bc)

    row16 = lax.broadcasted_iota(jnp.int32, (TILE, 128), 0)
    w_parts, keep_parts = [], []
    for s in range(2):
        first = firsts[s]
        inside = lax.rem(first, 128)
        loads[4 + s].wait()
        wt[s] = jnp.broadcast_to(walk_ref[s:s + 1, :], (128, 128)).T
        w_parts.append(wt[s, pl.ds(pl.multiple_of(inside, TILE), TILE), :])
        keep = (y * columns + first + row16) < NCOEF
        if s == 1:
            keep = keep & (jnp.full((TILE, 128), has_extra, jnp.int32) > 0)
        keep_parts.append(keep.astype(F32))

    loads[3].wait()
    for j in range(columns // 128):
        dt[j * 128:(j + 1) * 128, :] = d_ref[:, j * 128:(j + 1) * 128].T
    pl.semaphore_wait(barrier, 1 + 2 * len(hops4) + NZ - 1)

    def n_core(k, value):
        nc[k, core] = value
        push(nc.at[k, core], nc.at[k, core], nc_s.at[k], nc_r.at[k], sibling).start()
        sent(nc.at[k, 0], nc_s.at[k])

    def n_core_sum(k):
        received(nc.at[k, 0], nc_r.at[k])
        return nc[k, 0] + nc[k, 1]

    def n_x(k, value):
        nx[k, x] = value
        over_x(lambda x_: push(nx.at[k, x], nx.at[k, x], nx_s.at[k], nx_r.at[k], at(x_, z, core)).start())
        sent(nx.at[k, pl.ds(0, NX - 1)], nx_s.at[k])

    def n_x_sum(k):
        received(nx.at[k, pl.ds(0, NX - 1)], nx_r.at[k])
        return (nx[k, 0] + nx[k, 1]) + (nx[k, 2] + nx[k, 3])

    def n_z(k, value):
        nz[k, z] = value
        over_z(lambda z_: push(nz.at[k, z], nz.at[k, z], nz_s.at[k], nz_r.at[k], at(x, z_, core)).start())
        sent(nz.at[k, pl.ds(0, NZ - 1)], nz_s.at[k])

    def n_z_sum(k):
        received(nz.at[k, pl.ds(0, NZ - 1)], nz_r.at[k])
        return jnp.sum(nz[k], axis=0)

    def adjoint_piece(r, h, p):
        first = pl.multiple_of((h * NX + p) * piece, TILE)
        value = jnp.dot(dt[pl.ds(first, piece), :], u_ref[r], preferred_element_type=F32)
        return value.reshape(tiles, TILE, 128)

    def reduce_scatter(r, k, norm_value):
        n_core(k, norm_value)

        def theirs(i):
            p = wrap(x + nth(i, NX // 2), NX)
            cs[r, p] = adjoint_piece(r, 1 - core, p)
            push(cs.at[r, p], cr.at[r, p], cs_s.at[r], cs_r.at[r, p], sibling).start()
        loop(NX, theirs)
        sent(cs.at[r], cs_s.at[r])
        n_x(k, n_core_sum(k))

        def mine(p):
            value = adjoint_piece(r, core, p)
            received(cr.at[r, p], cs_r.at[r, p])
            return value + cr[r, p]

        def away(p):
            xs[r, p] = mine(p)
            half_away(p, 0)

        def half_away(p, h):
            push(xs.at[r, p, halves[h]], xr.at[r, x, halves[h]], xs_s.at[r], xs_r.at[r, h], at(p, z, core)).start()
        over_x(away)
        over_x(lambda p: half_away(p, 1))
        sent(xs.at[r, pl.ds(0, NX - 1)], xs_s.at[r])
        n_z(k, n_x_sum(k))
        xr[r, x] = mine(x)

        def elsewhere(e, act):
            pl.when(z != extra_owner(e, core))(act)

        for h in range(2):
            part = halves[h]
            received(xr.at[r, pl.ds(0, NX - 1), part], xs_r.at[r, h])
            tb[r, part] = (xr[r, 0, part] + xr[r, 1, part]) + (xr[r, 2, part] + xr[r, 3, part])
            if h == 1:
                for e in range(extras):
                    elsewhere(e, lambda e=e: push(
                        tb.at[r, NZ + e], zr.at[r, 1, z], ze_s.at[r, e], ze_r.at[r],
                        at(x, extra_owner(e, core), core)).start())

            def out_tile(z_, h=h):
                @pl.when((z_ >= SPLIT) if h else (z_ < SPLIT))
                def _():
                    push(tb.at[r, z_], zr.at[r, 0, z], zs_s.at[r], zs_r.at[r], at(x, z_, core)).start()
            over_z(out_tile)
        sent(tb.at[r, pl.ds(0, NZ - 1)], zs_s.at[r])
        zr[r, 0, z] = tb[r, z]

        def drain():
            for e in range(extras):
                elsewhere(e, lambda e=e: push(
                    tb.at[r, 0], tb.at[r, 0], ze_s.at[r, e], ze_s.at[r, e], sibling).wait_send())
        drains.append(drain)
        return n_z_sum(k)

    def owned(r, s):
        if s == 0:
            received(zr.at[r, 0, pl.ds(0, NZ - 1)], zs_r.at[r])
            return jnp.sum(zr[r, 0], axis=0) * keep_parts[0]
        own[r] = jnp.zeros((TILE, 128), F32)

        @pl.when(has_extra > 0)
        def _():
            zr[r, 1, z] = tb[r, NZ + which]
            received(zr.at[r, 1, pl.ds(0, NZ - 1)], ze_r.at[r])
            own[r] = jnp.sum(zr[r, 1], axis=0)
        return own[r] * keep_parts[1]

    def keep_tile(v, r, s, value):
        if s == 0:
            v[r, core, x, z] = value
        else:
            @pl.when(has_extra > 0)
            def _():
                v[r, core, x, NZ + which] = value

    def publish(v, r, q, s):
        many = v.at[r, core, x, pl.ds(0, NZ - 1)]
        if s == 0:
            main = v.at[r, core, x, z]
            over_z(lambda z_: push(main, main, az_s.at[q], az_r.at[q, late], at(x, z_, core)).start())
            sent(many, az_s.at[q])
            return

        @pl.when(has_extra > 0)
        def _():
            ref = v.at[r, core, x, NZ + which]
            over_z(lambda z_: push(ref, ref, ae_s.at[q], ae_r.at[q, which], at(x, z_, core)).start())

        def drain():
            @pl.when(has_extra > 0)
            def _():
                push(many, many, ae_s.at[q], ae_s.at[q], sibling).wait_send()
        drains.append(drain)

    def tiles_wait(v, r, q, h):
        count = NZ - SPLIT if h else SPLIT
        for inside in range(2):
            @pl.when(late == (h if inside else 1 - h))
            def _():
                received(v.at[r, core, x, pl.ds(0, count - inside)], az_r.at[q, h])
        if h == 1:
            for e in range(extras):
                @pl.when(z != extra_owner(e, core))
                def _():
                    received(v.at[r, core, x, 0], ae_r.at[q, e])

    def to_sibling(v, r, q, p, part):
        ref = v.at[r, core, p, part]
        push(ref, ref, ac_s.at[q], ac_r.at[q], sibling).start()

    def gather_x_start(v, r, q, part, h):
        ref = v.at[r, core, x, part]
        over_x(lambda x_: push(ref, ref, ax_s.at[q], ax_r.at[q, h, x], at(x_, z, core)).start())
        sent(v.at[r, core, pl.ds(0, NX - 1), part], ax_s.at[q])
        to_sibling(v, r, q, x, part)

    def gather_x_forward(v, r, q, part, h):
        for d in (1, 3, 2):
            p = x_peer(d)
            received(v.at[r, core, p, part], ax_r.at[q, h, p])
            to_sibling(v, r, q, p, part)
        sent(v.at[r, core, pl.ds(0, NX), part], ac_s.at[q])

    def gather_core_wait(v, r, q):
        received(v.at[r, 1 - core], ac_r.at[q])

    def rest_wait(r):
        for h in range(2):
            tiles_wait(vl, r, 2 * r + 1, h)

    def forward(r):
        value = vh[r].reshape(columns, 128)
        return jnp.dot(d_ref[...], value, preferred_element_type=F32) * mask_ref[...]

    def y_start(r, partial, norms):
        yb[r, y, :half] = partial
        yb[r, y, half:half + 8] = jnp.concatenate([norms, jnp.zeros((4, 128), F32)], axis=0)
        for d in hops4:
            push(yb.at[r, y], yb.at[r, y], y_s.at[r], y_r.at[r], y_peer(d)).start()
        sent(yb.at[r, pl.ds(0, NY - 1)], y_s.at[r])

    def y_wait(r):
        received(yb.at[r, pl.ds(0, NY - 1)], y_r.at[r])
        value = (yb[r, 0] + yb[r, 1]) + (yb[r, 2] + yb[r, 3])
        return value[:half], value[half:half + 4]

    def split(value):
        hi = value.astype(BF16)
        return hi, (value - hi.astype(F32)).astype(BF16)

    def gather(r, k, make, norms_of):
        values = []
        for s in range(2):
            value = make(s, owned(r, s))
            hi, lo = split(value)
            keep_tile(vh, r, s, hi)
            publish(vh, r, 2 * r, s)
            keep_tile(vl, r, s, lo)
            values.append(value)
        n_z(k, norms_of(values))
        for h in range(2):
            tiles_wait(vh, r, 2 * r, h)
            gather_x_start(vh, r, 2 * r, halves[h], h)
            if h == 0:
                n_x(k, n_z_sum(k))
        for h in range(2):
            gather_x_forward(vh, r, 2 * r, halves[h], h)
            if h == 0:
                n_core(k, n_x_sum(k))
        for s in range(2):
            publish(vl, r, 2 * r + 1, s)
        gather_core_wait(vh, r, 2 * r)
        return values, n_core_sum(k)

    def root(v):
        return jnp.sqrt(v + EPS)

    def walk_of(s, v):
        return w_parts[s] * (turn(v) - v)

    def totals(parts):
        return total(parts[0]) + total(parts[1])

    norm = reduce_scatter(0, 0, padded([total(bc * bc)]))
    beta1 = root(fold(norm[0:1]))

    def norms1(v):
        dv8 = [walk_of(s, v[s]) * 0.125 for s in range(2)]
        return padded([totals([e * e for e in v]), totals([e * e for e in dv8])])

    v1, norms = gather(0, 1, lambda s, got: got / beta1, norms1)
    y_start(0, compact(forward(0)), norms)
    image, norms = y_wait(0)

    alpha1 = root(fold(norms[0:1]))
    o2 = image / alpha1 - alpha1 * (bc_ref[...] / beta1)
    u_ref[1] = expand(o2)
    walk2 = (norms[1:2] / (alpha1 * alpha1)) * 64.0
    norm = reduce_scatter(1, 2, padded([total(o2 * o2)]))
    rest_wait(0)
    gather_x_start(vl, 0, 1, both, 0)
    beta2 = jnp.sqrt(fold(norm[0:1]) + walk2 + EPS)
    wz = [(walk_of(s, v1[s]) / alpha1) / beta2 for s in range(2)]

    def second_vector(s, got):
        return got / beta2 - w_parts[s] * wz[s] - beta2 * (v1[s] / alpha1)

    def norms2(v):
        dv8 = [walk_of(s, v[s]) * 0.125 for s in range(2)]
        return padded([
            totals([e * e for e in v]),
            totals([e * e for e in dv8]),
            totals([e * g for e, g in zip(dv8, wz)]),
            totals([g * g for g in wz]),
        ])

    v2, norms = gather(1, 3, second_vector, norms2)
    y_start(1, compact(forward(1)), norms)
    gather_x_forward(vl, 0, 1, both, 0)
    image, norms = y_wait(1)

    alpha2 = root(fold(norms[0:1]))
    o3 = image / alpha2 - alpha2 * (o2 / beta2)
    n_core(4, padded([total(o3 * o3)]))
    square = alpha2 * alpha2
    walk3 = (norms[1:2] / square) * 64.0 - 16.0 * norms[2:3] + square * norms[3:4]
    walk3 = jnp.maximum(walk3, 0.0)
    n_x(4, n_core_sum(4))
    n_z(4, n_x_sum(4))
    rest_wait(1)
    gather_x_start(vl, 1, 3, both, 0)
    gather_x_forward(vl, 1, 3, both, 0)
    rho1 = jnp.sqrt(alpha1 * alpha1 + beta2 * beta2)
    cos1, sin1 = alpha1 / rho1, beta2 / rho1
    first_step = cos1 * beta1 / rho1
    phi_bar = sin1 * beta1
    rho_bar = -cos1 * alpha2
    theta = sin1 * alpha2 / rho1
    gather_core_wait(vl, 0, 1)
    gather_core_wait(vl, 1, 3)
    beta3 = jnp.sqrt(fold(n_z_sum(4)[0:1]) + walk3 + EPS)
    rho2 = jnp.sqrt(rho_bar * rho_bar + beta3 * beta3)
    second_step = (rho_bar / rho2) * phi_bar / rho2
    weight1 = (first_step - second_step * theta) / alpha1
    weight2 = second_step / alpha2
    for c_ in range(NC):
        for p in range(NX):
            first = (vh[0, c_, p].astype(F32) + vl[0, c_, p].astype(F32)).reshape(piece, 128)
            second = (vh[1, c_, p].astype(F32) + vl[1, c_, p].astype(F32)).reshape(piece, 128)
            begin = (c_ * NX + p) * piece
            out[begin:begin + piece, :] = weight1 * first + weight2 * second

    for drain in drains:
        drain()


def body(design, observed, arc_lengths, arc_months, walk_weight):
    rows, columns = design.shape
    tiles = columns // (NC * NX * TILE)
    vmem = pl.BlockSpec(memory_space=pltpu.VMEM)
    hbm = pl.BlockSpec(memory_space=pltpu.HBM)
    dma = pltpu.SemaphoreType.DMA
    block = (tiles, TILE, 128)
    scratch = [
        pltpu.VMEM((rows, columns), BF16),
        pltpu.VMEM((columns, rows), BF16),
        pltpu.VMEM((observed.shape[1], rows), BF16),
        pltpu.SMEM(arc_lengths.shape, jnp.int32),
        pltpu.SMEM(arc_months.shape, jnp.int32),
        pltpu.VMEM((2, 128), F32),
        pltpu.VMEM((2, 128, 128), F32),
        pltpu.VMEM((rows, 128), F32),
        pltpu.VMEM((2, rows, 128), BF16),
        pltpu.VMEM((rows // 2, 128), F32),
        pltpu.VMEM((2, NX) + block, F32),
        pltpu.VMEM((2, NX) + block, F32),
        pltpu.VMEM((2, NX) + block, F32),
        pltpu.VMEM((2, NX) + block, F32),
        pltpu.VMEM((2,) + block, F32),
        pltpu.VMEM((2, 2, NZ, TILE, 128), F32),
        pltpu.VMEM((2, TILE, 128), F32),
        pltpu.VMEM((2, NC, NX) + block, BF16),
        pltpu.VMEM((2, NC, NX) + block, BF16),
        pltpu.VMEM((2, NY, rows // 2 + 8, 128), F32),
        pltpu.VMEM((5, NC, 4, 128), F32),
        pltpu.VMEM((5, NX, 4, 128), F32),
        pltpu.VMEM((5, NZ, 4, 128), F32),
        dma((6,)),
        dma((2,)), dma((2, NX)),
        dma((2,)), dma((2, 2)),
        dma((2,)), dma((2,)),
        dma((2, tiles - NZ)), dma((2,)),
        dma((4,)), dma((4, 2)),
        dma((4,)), dma((4, tiles - NZ)),
        dma((4,)), dma((4, 2, NX)),
        dma((4,)), dma((4,)),
        dma((2,)), dma((2,)),
        dma((5,)), dma((5,)),
        dma((5,)), dma((5,)),
        dma((5,)), dma((5,)),
    ]
    return pl.pallas_call(
        kernel,
        out_shape=jax.ShapeDtypeStruct((columns, 128), F32),
        in_specs=[hbm] * 5,
        out_specs=vmem,
        scratch_shapes=scratch,
        compiler_params=pltpu.CompilerParams(
            collective_id=0, has_side_effects=True, vmem_limit_bytes=63 * 1024 * 1024
        ),
    )(design, observed.T, arc_lengths, arc_months, walk_weight)


def solution(mesh):
    in_specs = (P("arcs", "coef"), P("arcs", None), P("arcs", None), P("arcs", None), P("coef"))
    return jax.shard_map(
        body, mesh=mesh, in_specs=in_specs, out_specs=P("coef", None), check_vma=False
    )
```

```python
import functools

import jax
import jax.numpy as jnp
from jax import lax
from jax.experimental import pallas as pl
from jax.experimental.pallas import tpu as pltpu
from jax.sharding import PartitionSpec as P

NCOEF = 9405
EPS = 1e-06
MESH = pl.DeviceIdType.MESH
NX, NZ, NC, NY = 4, 16, 2, 4
TILE = 16
SPLIT = 10
F32, BF16 = jnp.float32, jnp.bfloat16


def kernel(
    design, observed, lengths, months, walk, out,
    d_ref, dt, ob_ref, len_ref, mon_ref, walk_ref, wt, mask_ref, u_ref, bc_ref,
    cs, cr, xs, xr, tb, zr, own, vh, vl, yb, ng, nz, d2, second,
    in_sem, cs_s, cs_r, xs_s, xs_r, zs_s, zs_r, ze_s, ze_r,
    az_s, az_r, ae_s, ae_r, ax_s, ax_r, ac_s, ac_r, y_s, y_r,
    ng_s, ng_r, nz_s, nz_r,
):
    rows = d_ref.shape[0]
    columns = d_ref.shape[1]
    tiles = columns // (NC * NX * TILE)
    piece = tiles * TILE
    extras = tiles - NZ
    halves = (pl.ds(0, SPLIT), pl.ds(SPLIT, tiles - SPLIT))
    both = pl.ds(0, tiles)
    arc, y = lax.axis_index("arcs"), lax.axis_index("coef")
    core = lax.rem(arc, NC)
    z = lax.rem(arc // NC, NZ)
    x = arc // (NC * NZ)

    def at(x_, z_, c_):
        return ((x_ * NZ + z_) * NC + c_, y)

    def wrap(v, n):
        return lax.rem(v, n)

    sibling = at(x, z, 1 - core)
    hops4 = (2, 1, 3)

    def x_peer(d):
        return wrap(x + d, NX)

    def y_peer(d):
        return (arc, wrap(y + d, NY))

    def extra_owner(e, c_):
        return 3 * e + c_

    drains = []

    def push(src, dst, ssem, rsem, dev):
        return pltpu.make_async_remote_copy(
            src_ref=src, dst_ref=dst, send_sem=ssem, recv_sem=rsem,
            device_id=dev, device_id_type=MESH,
        )

    def sent(ref, sem):
        drains.append(push(ref, ref, sem, sem, sibling).wait_send)

    def received(ref, sem):
        push(ref, ref, sem, sem, sibling).wait_recv()

    def nth(i, middle):
        return middle + lax.div(i + 1, 2) * (1 - 2 * lax.rem(i, 2))

    def loop(count, body):
        def step(i, _):
            body(i)
            return 0
        lax.fori_loop(0, count, step, 0)

    def over_z(body):
        loop(NZ - 1, lambda i: body(wrap(z + nth(i, NZ // 2), NZ)))

    def over_x(body):
        loop(NX - 1, lambda i: body(wrap(x + nth(i, NX // 2), NX)))

    barrier = pltpu.get_barrier_semaphore()

    def greet(dev):
        pl.semaphore_signal(barrier, inc=1, device_id=dev, device_id_type=MESH)

    over_z(lambda z_: greet(at(x, z_, core)))
    for d in hops4:
        greet(at(x_peer(d), z, core))
        greet(at(x_peer(d), z, 1 - core))
        greet(y_peer(d))
    greet(sibling)

    has_extra = jnp.int32(0)
    which = jnp.int32(0)
    for e in range(extras):
        hit = (z == extra_owner(e, core)).astype(jnp.int32)
        has_extra = has_extra + hit
        which = which + e * hit
    late = (z >= SPLIT).astype(jnp.int32)
    base = (core * NX + x) * piece
    firsts = [base + z * TILE, base + (NZ + which) * TILE]

    loads = [
        pltpu.make_async_copy(src, dst, in_sem.at[i])
        for i, (src, dst) in enumerate([
            (lengths, len_ref), (months, mon_ref), (observed, ob_ref), (design, d_ref),
        ] + [
            (walk.at[pl.ds(pl.multiple_of(f // 128 * 128, 128), 128)], walk_ref.at[s])
            for s, f in enumerate(firsts)
        ])
    ]
    for load in loads:
        load.start()

    lane = lax.broadcasted_iota(jnp.int32, (rows, 128), 1)
    row = lax.broadcasted_iota(jnp.int32, (rows, 128), 0)
    start = jnp.int32(0)
    month_row = jnp.full((rows, 128), -1, jnp.int32)
    loads[0].wait()
    loads[1].wait()
    for j in range(len_ref.shape[1]):
        end = start + len_ref[0, j]
        month_row = jnp.where((row >= start) & (row < end), mon_ref[0, j], month_row)
        start = end
    side = (lane >= 64).astype(jnp.int32)
    mask_stack = (month_row == side).astype(F32)
    mask_ref[...] = mask_stack
    half = rows // 2
    low = lax.broadcasted_iota(jnp.int32, (half, 128), 1) < 64
    loads[2].wait()
    ob = ob_ref[...].astype(F32)
    ob = jnp.concatenate([ob, ob], axis=0).T * mask_stack

    def turn(v):
        return pltpu.roll(v, 64, 1)

    def compact(v):
        s = v + turn(v)
        return jnp.where(low, s[:half], s[half:])

    def expand(v):
        t = turn(v)
        first = jnp.where(low, v, t)
        second = jnp.where(low, t, v)
        return (jnp.concatenate([first, second], axis=0) * mask_ref[...]).astype(BF16)

    def fold(v):
        return v + turn(jnp.broadcast_to(v, (8, 128)))[:1]

    def total(v):
        return jnp.sum(v, axis=0, keepdims=True)

    def padded(parts):
        rest = 4 - len(parts)
        if rest:
            parts = parts + [jnp.zeros((rest, 128), F32)]
        return jnp.concatenate(parts, axis=0)

    bc = compact(ob)
    bc_ref[...] = bc
    u_ref[0] = expand(bc)

    row16 = lax.broadcasted_iota(jnp.int32, (TILE, 128), 0)
    w_parts, keep_parts = [], []
    for s in range(2):
        first = firsts[s]
        inside = lax.rem(first, 128)
        loads[4 + s].wait()
        wt[s] = jnp.broadcast_to(walk_ref[s:s + 1, :], (128, 128)).T
        w_parts.append(wt[s, pl.ds(pl.multiple_of(inside, TILE), TILE), :])
        keep = (y * columns + first + row16) < NCOEF
        if s == 1:
            keep = keep & (jnp.full((TILE, 128), has_extra, jnp.int32) > 0)
        keep_parts.append(keep.astype(F32))

    loads[3].wait()
    for j in range(columns // 128):
        dt[j * 128:(j + 1) * 128, :] = d_ref[:, j * 128:(j + 1) * 128].T
    for c_ in range(NC):
        d2[c_] = d_ref[:, c_ * (columns // NC):(c_ + 1) * (columns // NC)]

    def adjoint_piece(r, h, p):
        first = pl.multiple_of((h * NX + p) * piece, TILE)
        value = jnp.dot(dt[pl.ds(first, piece), :], u_ref[r], preferred_element_type=F32)
        return value.reshape(tiles, TILE, 128)

    pl.semaphore_wait(barrier, 1 + 3 * len(hops4) + NZ - 1)

    def n_group(k, value):
        slot = x * NC + core
        ng[k, slot] = value

        def give(x_, c_):
            push(ng.at[k, slot], ng.at[k, slot], ng_s.at[k], ng_r.at[k], at(x_, z, c_)).start()

        def give_both(x_):
            give(x_, core)
            give(x_, 1 - core)
        over_x(give_both)
        give(x, 1 - core)
        sent(ng.at[k, pl.ds(0, NX * NC - 1)], ng_s.at[k])

    def n_group_sum(k):
        received(ng.at[k, pl.ds(0, NX * NC - 1)], ng_r.at[k])
        return jnp.sum(ng[k], axis=0)

    def n_z(k, value):
        nz[k, z] = value
        over_z(lambda z_: push(nz.at[k, z], nz.at[k, z], nz_s.at[k], nz_r.at[k], at(x, z_, core)).start())
        sent(nz.at[k, pl.ds(0, NZ - 1)], nz_s.at[k])

    def n_z_sum(k):
        received(nz.at[k, pl.ds(0, NZ - 1)], nz_r.at[k])
        return jnp.sum(nz[k], axis=0)

    def reduce_scatter(r, k, norm_value):
        n_group(k, norm_value)

        def theirs(i):
            p = wrap(x + nth(i, NX // 2), NX)
            cs[r, p] = adjoint_piece(r, 1 - core, p)
            push(cs.at[r, p], cr.at[r, p], cs_s.at[r], cs_r.at[r, p], sibling).start()
        loop(NX, theirs)
        sent(cs.at[r], cs_s.at[r])

        def mine(p):
            value = adjoint_piece(r, core, p)
            received(cr.at[r, p], cs_r.at[r, p])
            return value + cr[r, p]

        def away(p):
            xs[r, p] = mine(p)
            half_away(p, 0)

        def half_away(p, h):
            push(xs.at[r, p, halves[h]], xr.at[r, x, halves[h]], xs_s.at[r], xs_r.at[r, h], at(p, z, core)).start()
        over_x(away)
        over_x(lambda p: half_away(p, 1))
        sent(xs.at[r, pl.ds(0, NX - 1)], xs_s.at[r])
        n_z(k, n_group_sum(k))
        xr[r, x] = mine(x)

        def elsewhere(e, act):
            pl.when(z != extra_owner(e, core))(act)

        for h in range(2):
            part = halves[h]
            received(xr.at[r, pl.ds(0, NX - 1), part], xs_r.at[r, h])
            tb[r, part] = (xr[r, 0, part] + xr[r, 1, part]) + (xr[r, 2, part] + xr[r, 3, part])
            if h == 1:
                for e in range(extras):
                    elsewhere(e, lambda e=e: push(
                        tb.at[r, NZ + e], zr.at[r, 1, z], ze_s.at[r, e], ze_r.at[r],
                        at(x, extra_owner(e, core), core)).start())

            def out_tile(z_, h=h):
                @pl.when((z_ >= SPLIT) if h else (z_ < SPLIT))
                def _():
                    push(tb.at[r, z_], zr.at[r, 0, z], zs_s.at[r], zs_r.at[r], at(x, z_, core)).start()
            over_z(out_tile)
        sent(tb.at[r, pl.ds(0, NZ - 1)], zs_s.at[r])
        zr[r, 0, z] = tb[r, z]

        def drain():
            for e in range(extras):
                elsewhere(e, lambda e=e: push(
                    tb.at[r, 0], tb.at[r, 0], ze_s.at[r, e], ze_s.at[r, e], sibling).wait_send())
        drains.append(drain)
        return n_z_sum(k)

    def owned(r, s):
        if s == 0:
            received(zr.at[r, 0, pl.ds(0, NZ - 1)], zs_r.at[r])
            return jnp.sum(zr[r, 0], axis=0) * keep_parts[0]
        own[r] = jnp.zeros((TILE, 128), F32)

        @pl.when(has_extra > 0)
        def _():
            zr[r, 1, z] = tb[r, NZ + which]
            received(zr.at[r, 1, pl.ds(0, NZ - 1)], ze_r.at[r])
            own[r] = jnp.sum(zr[r, 1], axis=0)
        return own[r] * keep_parts[1]

    def keep_tile(v, r, s, value):
        if s == 0:
            v[r, core, x, z] = value
        else:
            @pl.when(has_extra > 0)
            def _():
                v[r, core, x, NZ + which] = value

    def publish(v, r, q, s):
        many = v.at[r, core, x, pl.ds(0, NZ - 1)]
        if s == 0:
            main = v.at[r, core, x, z]
            over_z(lambda z_: push(main, main, az_s.at[q], az_r.at[q, late], at(x, z_, core)).start())
            sent(many, az_s.at[q])
            return

        @pl.when(has_extra > 0)
        def _():
            ref = v.at[r, core, x, NZ + which]
            over_z(lambda z_: push(ref, ref, ae_s.at[q], ae_r.at[q, which], at(x, z_, core)).start())

        def drain():
            @pl.when(has_extra > 0)
            def _():
                push(many, many, ae_s.at[q], ae_s.at[q], sibling).wait_send()
        drains.append(drain)

    def tiles_wait(v, r, q, h):
        count = NZ - SPLIT if h else SPLIT
        for inside in range(2):
            @pl.when(late == (h if inside else 1 - h))
            def _():
                received(v.at[r, core, x, pl.ds(0, count - inside)], az_r.at[q, h])
        if h == 1:
            for e in range(extras):
                @pl.when(z != extra_owner(e, core))
                def _():
                    received(v.at[r, core, x, 0], ae_r.at[q, e])

    def to_sibling(v, r, q, p, part):
        ref = v.at[r, core, p, part]
        push(ref, ref, ac_s.at[q], ac_r.at[q], sibling).start()

    def gather_x_start(v, r, q, part, h):
        ref = v.at[r, core, x, part]
        over_x(lambda x_: push(ref, ref, ax_s.at[q], ax_r.at[q, h, x], at(x_, z, core)).start())
        sent(v.at[r, core, pl.ds(0, NX - 1), part], ax_s.at[q])
        to_sibling(v, r, q, x, part)

    def gather_x_forward(v, r, q, part, h):
        for d in (1, 3, 2):
            p = x_peer(d)
            received(v.at[r, core, p, part], ax_r.at[q, h, p])
            to_sibling(v, r, q, p, part)
        sent(v.at[r, core, pl.ds(0, NX), part], ac_s.at[q])

    def gather_core_wait(v, r, q):
        received(v.at[r, 1 - core], ac_r.at[q])

    def rest_wait(r):
        for h in range(2):
            tiles_wait(vl, r, 2 * r + 1, h)

    def forward(r, c_):
        value = vh[r, c_].reshape(columns // NC, 128)
        return jnp.dot(d2[c_], value, preferred_element_type=F32)

    def y_start(r, partial, norms):
        yb[r, y, :half] = partial
        yb[r, y, half:half + 8] = jnp.concatenate([norms, jnp.zeros((4, 128), F32)], axis=0)
        for d in hops4:
            push(yb.at[r, y], yb.at[r, y], y_s.at[r], y_r.at[r], y_peer(d)).start()
        sent(yb.at[r, pl.ds(0, NY - 1)], y_s.at[r])

    def y_wait(r):
        received(yb.at[r, pl.ds(0, NY - 1)], y_r.at[r])
        value = (yb[r, 0] + yb[r, 1]) + (yb[r, 2] + yb[r, 3])
        return value[:half], value[half:half + 4]

    def split(value):
        hi = value.astype(BF16)
        return hi, (value - hi.astype(F32)).astype(BF16)

    def gather(r, k, make, norms_of):
        values = []
        for s in range(2):
            value = make(s, owned(r, s))
            hi, lo = split(value)
            keep_tile(vh, r, s, hi)
            publish(vh, r, 2 * r, s)
            keep_tile(vl, r, s, lo)
            values.append(value)
        n_z(k, norms_of(values))
        for h in range(2):
            tiles_wait(vh, r, 2 * r, h)
            gather_x_start(vh, r, 2 * r, halves[h], h)
        n_group(k, n_z_sum(k))
        for s in range(2):
            publish(vl, r, 2 * r + 1, s)
        for h in range(2):
            gather_x_forward(vh, r, 2 * r, halves[h], h)
        image = forward(r, core)
        gather_core_wait(vh, r, 2 * r)
        image = image + forward(r, 1 - core)
        y_start(r, compact(image * mask_ref[...]), n_group_sum(k))
        rest_wait(r)
        gather_x_start(vl, r, 2 * r + 1, both, 0)
        return values

    def root(v):
        return jnp.sqrt(v + EPS)

    def walk_of(s, v):
        return w_parts[s] * (turn(v) - v)

    def totals(parts):
        return total(parts[0]) + total(parts[1])

    norm = reduce_scatter(0, 0, padded([total(bc * bc)]))
    beta1 = root(fold(norm[0:1]))

    def norms1(v):
        dv8 = [walk_of(s, v[s]) * 0.125 for s in range(2)]
        return padded([totals([e * e for e in v]), totals([e * e for e in dv8])])

    v1 = gather(0, 1, lambda s, got: got / beta1, norms1)
    image, norms = y_wait(0)

    alpha1 = root(fold(norms[0:1]))
    o2 = image / alpha1 - alpha1 * (bc_ref[...] / beta1)
    u_ref[1] = expand(o2)
    walk2 = (norms[1:2] / (alpha1 * alpha1)) * 64.0
    norm = reduce_scatter(1, 2, padded([total(o2 * o2)]))
    beta2 = jnp.sqrt(fold(norm[0:1]) + walk2 + EPS)
    wz = [(walk_of(s, v1[s]) / alpha1) / beta2 for s in range(2)]

    def second_vector(s, got):
        return got / beta2 - w_parts[s] * wz[s] - beta2 * (v1[s] / alpha1)

    def norms2(v):
        dv8 = [walk_of(s, v[s]) * 0.125 for s in range(2)]
        return padded([
            totals([e * e for e in v]),
            totals([e * e for e in dv8]),
            totals([e * g for e, g in zip(dv8, wz)]),
            totals([g * g for g in wz]),
        ])

    v2 = gather(1, 3, second_vector, norms2)
    gather_x_forward(vl, 0, 1, both, 0)
    image, norms = y_wait(1)

    alpha2 = root(fold(norms[0:1]))
    o3 = image / alpha2 - alpha2 * (o2 / beta2)
    n_group(4, padded([total(o3 * o3)]))
    square = alpha2 * alpha2
    walk3 = (norms[1:2] / square) * 64.0 - 16.0 * norms[2:3] + square * norms[3:4]
    walk3 = jnp.maximum(walk3, 0.0)
    n_z(4, n_group_sum(4))
    gather_x_forward(vl, 1, 3, both, 0)
    rho1 = jnp.sqrt(alpha1 * alpha1 + beta2 * beta2)
    cos1, sin1 = alpha1 / rho1, beta2 / rho1
    first_step = cos1 * beta1 / rho1
    phi_bar = sin1 * beta1
    rho_bar = -cos1 * alpha2
    theta = sin1 * alpha2 / rho1
    gather_core_wait(vl, 0, 1)
    gather_core_wait(vl, 1, 3)
    for c_ in range(NC):
        for p in range(NX):
            begin = (c_ * NX + p) * piece
            for r, target in ((0, out), (1, second)):
                value = vh[r, c_, p].astype(F32) + vl[r, c_, p].astype(F32)
                target[begin:begin + piece, :] = value.reshape(piece, 128)
    beta3 = jnp.sqrt(fold(n_z_sum(4)[0:1]) + walk3 + EPS)
    rho2 = jnp.sqrt(rho_bar * rho_bar + beta3 * beta3)
    second_step = (rho_bar / rho2) * phi_bar / rho2
    weight1 = (first_step - second_step * theta) / alpha1
    weight2 = second_step / alpha2
    out[...] = weight1 * out[...] + weight2 * second[...]

    for drain in drains:
        drain()


def body(design, observed, arc_lengths, arc_months, walk_weight):
    rows, columns = design.shape
    tiles = columns // (NC * NX * TILE)
    vmem = pl.BlockSpec(memory_space=pltpu.VMEM)
    hbm = pl.BlockSpec(memory_space=pltpu.HBM)
    dma = pltpu.SemaphoreType.DMA
    block = (tiles, TILE, 128)
    scratch = [
        pltpu.VMEM((rows, columns), BF16),
        pltpu.VMEM((columns, rows), BF16),
        pltpu.VMEM((observed.shape[1], rows), BF16),
        pltpu.SMEM(arc_lengths.shape, jnp.int32),
        pltpu.SMEM(arc_months.shape, jnp.int32),
        pltpu.VMEM((2, 128), F32),
        pltpu.VMEM((2, 128, 128), F32),
        pltpu.VMEM((rows, 128), F32),
        pltpu.VMEM((2, rows, 128), BF16),
        pltpu.VMEM((rows // 2, 128), F32),
        pltpu.VMEM((2, NX) + block, F32),
        pltpu.VMEM((2, NX) + block, F32),
        pltpu.VMEM((2, NX) + block, F32),
        pltpu.VMEM((2, NX) + block, F32),
        pltpu.VMEM((2,) + block, F32),
        pltpu.VMEM((2, 2, NZ, TILE, 128), F32),
        pltpu.VMEM((2, TILE, 128), F32),
        pltpu.VMEM((2, NC, NX) + block, BF16),
        pltpu.VMEM((2, NC, NX) + block, BF16),
        pltpu.VMEM((2, NY, rows // 2 + 8, 128), F32),
        pltpu.VMEM((5, NX * NC, 4, 128), F32),
        pltpu.VMEM((5, NZ, 4, 128), F32),
        pltpu.VMEM((NC, rows, columns // NC), BF16),
        pltpu.VMEM((columns, 128), F32),
        dma((6,)),
        dma((2,)), dma((2, NX)),
        dma((2,)), dma((2, 2)),
        dma((2,)), dma((2,)),
        dma((2, tiles - NZ)), dma((2,)),
        dma((4,)), dma((4, 2)),
        dma((4,)), dma((4, tiles - NZ)),
        dma((4,)), dma((4, 2, NX)),
        dma((4,)), dma((4,)),
        dma((2,)), dma((2,)),
        dma((5,)), dma((5,)),
        dma((5,)), dma((5,)),
    ]
    return pl.pallas_call(
        kernel,
        out_shape=jax.ShapeDtypeStruct((columns, 128), F32),
        in_specs=[hbm] * 5,
        out_specs=vmem,
        scratch_shapes=scratch,
        compiler_params=pltpu.CompilerParams(
            collective_id=0, has_side_effects=True, vmem_limit_bytes=63 * 1024 * 1024
        ),
    )(design, observed.T, arc_lengths, arc_months, walk_weight)


def solution(mesh):
    in_specs = (P("arcs", "coef"), P("arcs", None), P("arcs", None), P("arcs", None), P("coef"))
    return jax.shard_map(
        body, mesh=mesh, in_specs=in_specs, out_specs=P("coef", None), check_vma=False
    )
```

```python
import functools

import jax
import jax.numpy as jnp
from jax import lax
from jax.experimental import pallas as pl
from jax.experimental.pallas import tpu as pltpu
from jax.sharding import PartitionSpec as P

NCOEF = 9405
EPS = 1e-06
MESH = pl.DeviceIdType.MESH
NX, NZ, NC, NY = 4, 16, 2, 4
TILE = 16
SPLIT = 10
F32, BF16 = jnp.float32, jnp.bfloat16


def kernel(
    design, observed, lengths, months, walk, out,
    d_ref, dt, ob_ref, len_ref, mon_ref, walk_ref, wt, mask_ref, u_ref, bc_ref,
    cs, cr, xs, xr, tb, zr, own, vh, vl, yb, ng, nz, d2, second,
    in_sem, cs_s, cs_r, xs_s, xs_r, zs_s, zs_r, ze_s, ze_r,
    az_s, az_r, ae_s, ae_r, ax_s, ax_r, ac_s, ac_r, y_s, y_r,
    ng_s, ng_r, nz_s, nz_r,
):
    rows = d_ref.shape[0]
    columns = d_ref.shape[1]
    tiles = columns // (NC * NX * TILE)
    piece = tiles * TILE
    extras = tiles - NZ
    halves = (pl.ds(0, SPLIT), pl.ds(SPLIT, tiles - SPLIT))
    both = pl.ds(0, tiles)
    arc, y = lax.axis_index("arcs"), lax.axis_index("coef")
    core = lax.rem(arc, NC)
    z = lax.rem(arc // NC, NZ)
    x = arc // (NC * NZ)

    def at(x_, z_, c_):
        return ((x_ * NZ + z_) * NC + c_, y)

    def wrap(v, n):
        return lax.rem(v, n)

    sibling = at(x, z, 1 - core)
    hops4 = (2, 1, 3)

    def x_peer(d):
        return wrap(x + d, NX)

    def y_peer(d):
        return (arc, wrap(y + d, NY))

    def extra_owner(e, c_):
        return 3 * e + c_

    drains = []

    def push(src, dst, ssem, rsem, dev):
        return pltpu.make_async_remote_copy(
            src_ref=src, dst_ref=dst, send_sem=ssem, recv_sem=rsem,
            device_id=dev, device_id_type=MESH,
        )

    def sent(ref, sem):
        drains.append(push(ref, ref, sem, sem, sibling).wait_send)

    def received(ref, sem):
        push(ref, ref, sem, sem, sibling).wait_recv()

    def nth(i, middle):
        return middle + lax.div(i + 1, 2) * (1 - 2 * lax.rem(i, 2))

    def loop(count, body):
        def step(i, _):
            body(i)
            return 0
        lax.fori_loop(0, count, step, 0)

    def over_z(body):
        loop(NZ - 1, lambda i: body(wrap(z + nth(i, NZ // 2), NZ)))

    def over_x(body):
        loop(NX - 1, lambda i: body(wrap(x + nth(i, NX // 2), NX)))

    barrier = pltpu.get_barrier_semaphore()

    def greet(dev):
        pl.semaphore_signal(barrier, inc=1, device_id=dev, device_id_type=MESH)

    over_z(lambda z_: greet(at(x, z_, core)))
    for d in hops4:
        greet(at(x_peer(d), z, core))
        greet(at(x_peer(d), z, 1 - core))
        greet(y_peer(d))
    greet(sibling)

    has_extra = jnp.int32(0)
    which = jnp.int32(0)
    for e in range(extras):
        hit = (z == extra_owner(e, core)).astype(jnp.int32)
        has_extra = has_extra + hit
        which = which + e * hit
    late = (z >= SPLIT).astype(jnp.int32)
    base = (core * NX + x) * piece
    firsts = [base + z * TILE, base + (NZ + which) * TILE]

    loads = [
        pltpu.make_async_copy(src, dst, in_sem.at[i])
        for i, (src, dst) in enumerate([
            (lengths, len_ref), (months, mon_ref), (observed, ob_ref), (design, d_ref),
        ] + [
            (walk.at[pl.ds(pl.multiple_of(f // 128 * 128, 128), 128)], walk_ref.at[s])
            for s, f in enumerate(firsts)
        ])
    ]
    for load in loads:
        load.start()

    lane = lax.broadcasted_iota(jnp.int32, (rows, 128), 1)
    row = lax.broadcasted_iota(jnp.int32, (rows, 128), 0)
    start = jnp.int32(0)
    month_row = jnp.full((rows, 128), -1, jnp.int32)
    loads[0].wait()
    loads[1].wait()
    for j in range(len_ref.shape[1]):
        end = start + len_ref[0, j]
        month_row = jnp.where((row >= start) & (row < end), mon_ref[0, j], month_row)
        start = end
    side = (lane >= 64).astype(jnp.int32)
    mask_stack = (month_row == side).astype(F32)
    mask_ref[...] = mask_stack
    half = rows // 2
    low = lax.broadcasted_iota(jnp.int32, (half, 128), 1) < 64
    loads[2].wait()
    ob = ob_ref[...].astype(F32)
    ob = jnp.concatenate([ob, ob], axis=0).T * mask_stack

    def turn(v):
        return pltpu.roll(v, 64, 1)

    def compact(v):
        s = v + turn(v)
        return jnp.where(low, s[:half], s[half:])

    def expand(v):
        t = turn(v)
        first = jnp.where(low, v, t)
        second = jnp.where(low, t, v)
        return (jnp.concatenate([first, second], axis=0) * mask_ref[...]).astype(BF16)

    def fold(v):
        return v + turn(jnp.broadcast_to(v, (8, 128)))[:1]

    def total(v):
        return jnp.sum(v, axis=0, keepdims=True)

    def padded(parts):
        rest = 4 - len(parts)
        if rest:
            parts = parts + [jnp.zeros((rest, 128), F32)]
        return jnp.concatenate(parts, axis=0)

    bc = compact(ob)
    bc_ref[...] = bc
    u_ref[0] = expand(bc)

    row16 = lax.broadcasted_iota(jnp.int32, (TILE, 128), 0)
    w_parts, keep_parts = [], []
    for s in range(2):
        first = firsts[s]
        inside = lax.rem(first, 128)
        loads[4 + s].wait()
        wt[s] = jnp.broadcast_to(walk_ref[s:s + 1, :], (128, 128)).T
        w_parts.append(wt[s, pl.ds(pl.multiple_of(inside, TILE), TILE), :])
        keep = (y * columns + first + row16) < NCOEF
        if s == 1:
            keep = keep & (jnp.full((TILE, 128), has_extra, jnp.int32) > 0)
        keep_parts.append(keep.astype(F32))

    loads[3].wait()
    for j in range(columns // 128):
        dt[j * 128:(j + 1) * 128, :] = d_ref[:, j * 128:(j + 1) * 128].T
    for c_ in range(NC):
        d2[c_] = d_ref[:, c_ * (columns // NC):(c_ + 1) * (columns // NC)]

    def adjoint_piece(r, h, p):
        first = pl.multiple_of((h * NX + p) * piece, TILE)
        value = jnp.dot(dt[pl.ds(first, piece), :], u_ref[r], preferred_element_type=F32)
        return value.reshape(tiles, TILE, 128)

    pl.semaphore_wait(barrier, 1 + 3 * len(hops4) + NZ - 1)

    def n_group(k, value):
        slot = x * NC + core
        ng[k, slot] = value

        def give(x_, c_):
            push(ng.at[k, slot], ng.at[k, slot], ng_s.at[k], ng_r.at[k], at(x_, z, c_)).start()

        def give_both(x_):
            give(x_, core)
            give(x_, 1 - core)
        over_x(give_both)
        give(x, 1 - core)
        sent(ng.at[k, pl.ds(0, NX * NC - 1)], ng_s.at[k])

    def n_group_sum(k):
        received(ng.at[k, pl.ds(0, NX * NC - 1)], ng_r.at[k])
        return jnp.sum(ng[k], axis=0)

    def n_z(k, value):
        nz[k, z] = value
        over_z(lambda z_: push(nz.at[k, z], nz.at[k, z], nz_s.at[k], nz_r.at[k], at(x, z_, core)).start())
        sent(nz.at[k, pl.ds(0, NZ - 1)], nz_s.at[k])

    def n_z_sum(k):
        received(nz.at[k, pl.ds(0, NZ - 1)], nz_r.at[k])
        return jnp.sum(nz[k], axis=0)

    def reduce_scatter(r, k, norm_value):
        n_group(k, norm_value)

        def theirs(i):
            p = wrap(x + nth(i, NX // 2), NX)
            cs[r, p] = adjoint_piece(r, 1 - core, p)
            push(cs.at[r, p], cr.at[r, p], cs_s.at[r], cs_r.at[r, p], sibling).start()
        loop(NX, theirs)
        sent(cs.at[r], cs_s.at[r])

        def mine(p):
            value = adjoint_piece(r, core, p)
            received(cr.at[r, p], cs_r.at[r, p])
            return value + cr[r, p]

        def away(p):
            xs[r, p] = mine(p)
            half_away(p, 0)

        def half_away(p, h):
            push(xs.at[r, p, halves[h]], xr.at[r, x, halves[h]], xs_s.at[r], xs_r.at[r, h], at(p, z, core)).start()
        over_x(away)
        over_x(lambda p: half_away(p, 1))
        sent(xs.at[r, pl.ds(0, NX - 1)], xs_s.at[r])
        n_z(k, n_group_sum(k))
        xr[r, x] = mine(x)

        def elsewhere(e, act):
            pl.when(z != extra_owner(e, core))(act)

        for h in range(2):
            part = halves[h]
            received(xr.at[r, pl.ds(0, NX - 1), part], xs_r.at[r, h])
            tb[r, part] = (xr[r, 0, part] + xr[r, 1, part]) + (xr[r, 2, part] + xr[r, 3, part])

            def out_tile(z_, h=h):
                @pl.when((z_ >= SPLIT) if h else (z_ < SPLIT))
                def _():
                    push(tb.at[r, z_], zr.at[r, 0, z], zs_s.at[r], zs_r.at[r], at(x, z_, core)).start()
            over_z(out_tile)
            if h == 1:
                for e in range(extras):
                    elsewhere(e, lambda e=e: push(
                        tb.at[r, NZ + e], zr.at[r, 1, z], ze_s.at[r, e], ze_r.at[r],
                        at(x, extra_owner(e, core), core)).start())
        sent(tb.at[r, pl.ds(0, NZ - 1)], zs_s.at[r])
        zr[r, 0, z] = tb[r, z]

        def drain():
            for e in range(extras):
                elsewhere(e, lambda e=e: push(
                    tb.at[r, 0], tb.at[r, 0], ze_s.at[r, e], ze_s.at[r, e], sibling).wait_send())
        drains.append(drain)
        return n_z_sum(k)

    def owned(r, s):
        if s == 0:
            received(zr.at[r, 0, pl.ds(0, NZ - 1)], zs_r.at[r])
            return jnp.sum(zr[r, 0], axis=0) * keep_parts[0]
        own[r] = jnp.zeros((TILE, 128), F32)

        @pl.when(has_extra > 0)
        def _():
            zr[r, 1, z] = tb[r, NZ + which]
            received(zr.at[r, 1, pl.ds(0, NZ - 1)], ze_r.at[r])
            own[r] = jnp.sum(zr[r, 1], axis=0)
        return own[r] * keep_parts[1]

    def keep_tile(v, r, s, value):
        if s == 0:
            v[r, core, x, z] = value
        else:
            @pl.when(has_extra > 0)
            def _():
                v[r, core, x, NZ + which] = value

    def publish(v, r, q, s):
        many = v.at[r, core, x, pl.ds(0, NZ - 1)]
        if s == 0:
            main = v.at[r, core, x, z]
            over_z(lambda z_: push(main, main, az_s.at[q], az_r.at[q, late], at(x, z_, core)).start())
            sent(many, az_s.at[q])
            return

        @pl.when(has_extra > 0)
        def _():
            ref = v.at[r, core, x, NZ + which]
            over_z(lambda z_: push(ref, ref, ae_s.at[q], ae_r.at[q, which], at(x, z_, core)).start())

        def drain():
            @pl.when(has_extra > 0)
            def _():
                push(many, many, ae_s.at[q], ae_s.at[q], sibling).wait_send()
        drains.append(drain)

    def tiles_wait(v, r, q, h):
        count = NZ - SPLIT if h else SPLIT
        for inside in range(2):
            @pl.when(late == (h if inside else 1 - h))
            def _():
                received(v.at[r, core, x, pl.ds(0, count - inside)], az_r.at[q, h])
        if h == 1:
            for e in range(extras):
                @pl.when(z != extra_owner(e, core))
                def _():
                    received(v.at[r, core, x, 0], ae_r.at[q, e])

    def to_sibling(v, r, q, p, part):
        ref = v.at[r, core, p, part]
        push(ref, ref, ac_s.at[q], ac_r.at[q], sibling).start()

    def gather_x_start(v, r, q, part, h):
        ref = v.at[r, core, x, part]
        over_x(lambda x_: push(ref, ref, ax_s.at[q], ax_r.at[q, h, x], at(x_, z, core)).start())
        sent(v.at[r, core, pl.ds(0, NX - 1), part], ax_s.at[q])
        to_sibling(v, r, q, x, part)

    def gather_x_forward(v, r, q, part, h):
        for d in (1, 3, 2):
            p = x_peer(d)
            received(v.at[r, core, p, part], ax_r.at[q, h, p])
            to_sibling(v, r, q, p, part)
        sent(v.at[r, core, pl.ds(0, NX), part], ac_s.at[q])

    def gather_core_wait(v, r, q):
        received(v.at[r, 1 - core], ac_r.at[q])

    def rest_wait(r):
        for h in range(2):
            tiles_wait(vl, r, 2 * r + 1, h)

    def forward(r, c_):
        value = vh[r, c_].reshape(columns // NC, 128)
        return jnp.dot(d2[c_], value, preferred_element_type=F32)

    def y_start(r, partial, norms):
        yb[r, y, :half] = partial
        yb[r, y, half:half + 8] = jnp.concatenate([norms, jnp.zeros((4, 128), F32)], axis=0)
        for d in hops4:
            push(yb.at[r, y], yb.at[r, y], y_s.at[r], y_r.at[r], y_peer(d)).start()
        sent(yb.at[r, pl.ds(0, NY - 1)], y_s.at[r])

    def y_wait(r):
        received(yb.at[r, pl.ds(0, NY - 1)], y_r.at[r])
        value = (yb[r, 0] + yb[r, 1]) + (yb[r, 2] + yb[r, 3])
        return value[:half], value[half:half + 4]

    def split(value):
        hi = value.astype(BF16)
        return hi, (value - hi.astype(F32)).astype(BF16)

    def gather(r, k, make, norms_of):
        values = []
        for s in range(2):
            value = make(s, owned(r, s))
            hi, lo = split(value)
            keep_tile(vh, r, s, hi)
            publish(vh, r, 2 * r, s)
            keep_tile(vl, r, s, lo)
            values.append(value)
        n_z(k, norms_of(values))
        for h in range(2):
            tiles_wait(vh, r, 2 * r, h)
            gather_x_start(vh, r, 2 * r, halves[h], h)
        n_group(k, n_z_sum(k))
        for s in range(2):
            publish(vl, r, 2 * r + 1, s)
        for h in range(2):
            gather_x_forward(vh, r, 2 * r, halves[h], h)
        image = forward(r, core)
        gather_core_wait(vh, r, 2 * r)
        image = image + forward(r, 1 - core)
        y_start(r, compact(image * mask_ref[...]), n_group_sum(k))
        rest_wait(r)
        gather_x_start(vl, r, 2 * r + 1, both, 0)
        return values

    def root(v):
        return jnp.sqrt(v + EPS)

    def walk_of(s, v):
        return w_parts[s] * (turn(v) - v)

    def totals(parts):
        return total(parts[0]) + total(parts[1])

    norm = reduce_scatter(0, 0, padded([total(bc * bc)]))
    beta1 = root(fold(norm[0:1]))

    def norms1(v):
        dv8 = [walk_of(s, v[s]) * 0.125 for s in range(2)]
        return padded([totals([e * e for e in v]), totals([e * e for e in dv8])])

    v1 = gather(0, 1, lambda s, got: got / beta1, norms1)
    image, norms = y_wait(0)

    alpha1 = root(fold(norms[0:1]))
    o2 = image / alpha1 - alpha1 * (bc_ref[...] / beta1)
    u_ref[1] = expand(o2)
    walk2 = (norms[1:2] / (alpha1 * alpha1)) * 64.0
    norm = reduce_scatter(1, 2, padded([total(o2 * o2)]))
    beta2 = jnp.sqrt(fold(norm[0:1]) + walk2 + EPS)
    wz = [(walk_of(s, v1[s]) / alpha1) / beta2 for s in range(2)]

    def second_vector(s, got):
        return got / beta2 - w_parts[s] * wz[s] - beta2 * (v1[s] / alpha1)

    def norms2(v):
        dv8 = [walk_of(s, v[s]) * 0.125 for s in range(2)]
        return padded([
            totals([e * e for e in v]),
            totals([e * e for e in dv8]),
            totals([e * g for e, g in zip(dv8, wz)]),
            totals([g * g for g in wz]),
        ])

    v2 = gather(1, 3, second_vector, norms2)
    gather_x_forward(vl, 0, 1, both, 0)
    image, norms = y_wait(1)

    alpha2 = root(fold(norms[0:1]))
    o3 = image / alpha2 - alpha2 * (o2 / beta2)
    n_group(4, padded([total(o3 * o3)]))
    square = alpha2 * alpha2
    walk3 = (norms[1:2] / square) * 64.0 - 16.0 * norms[2:3] + square * norms[3:4]
    walk3 = jnp.maximum(walk3, 0.0)
    n_z(4, n_group_sum(4))
    gather_x_forward(vl, 1, 3, both, 0)
    rho1 = jnp.sqrt(alpha1 * alpha1 + beta2 * beta2)
    cos1, sin1 = alpha1 / rho1, beta2 / rho1
    first_step = cos1 * beta1 / rho1
    phi_bar = sin1 * beta1
    rho_bar = -cos1 * alpha2
    theta = sin1 * alpha2 / rho1
    gather_core_wait(vl, 0, 1)
    gather_core_wait(vl, 1, 3)
    for c_ in range(NC):
        for p in range(NX):
            begin = (c_ * NX + p) * piece
            for r, target in ((0, out), (1, second)):
                value = vh[r, c_, p].astype(F32) + vl[r, c_, p].astype(F32)
                target[begin:begin + piece, :] = value.reshape(piece, 128)
    beta3 = jnp.sqrt(fold(n_z_sum(4)[0:1]) + walk3 + EPS)
    rho2 = jnp.sqrt(rho_bar * rho_bar + beta3 * beta3)
    second_step = (rho_bar / rho2) * phi_bar / rho2
    weight1 = (first_step - second_step * theta) / alpha1
    weight2 = second_step / alpha2
    out[...] = weight1 * out[...] + weight2 * second[...]

    for drain in drains:
        drain()


def body(design, observed, arc_lengths, arc_months, walk_weight):
    rows, columns = design.shape
    tiles = columns // (NC * NX * TILE)
    vmem = pl.BlockSpec(memory_space=pltpu.VMEM)
    hbm = pl.BlockSpec(memory_space=pltpu.HBM)
    dma = pltpu.SemaphoreType.DMA
    block = (tiles, TILE, 128)
    scratch = [
        pltpu.VMEM((rows, columns), BF16),
        pltpu.VMEM((columns, rows), BF16),
        pltpu.VMEM((observed.shape[1], rows), BF16),
        pltpu.SMEM(arc_lengths.shape, jnp.int32),
        pltpu.SMEM(arc_months.shape, jnp.int32),
        pltpu.VMEM((2, 128), F32),
        pltpu.VMEM((2, 128, 128), F32),
        pltpu.VMEM((rows, 128), F32),
        pltpu.VMEM((2, rows, 128), BF16),
        pltpu.VMEM((rows // 2, 128), F32),
        pltpu.VMEM((2, NX) + block, F32),
        pltpu.VMEM((2, NX) + block, F32),
        pltpu.VMEM((2, NX) + block, F32),
        pltpu.VMEM((2, NX) + block, F32),
        pltpu.VMEM((2,) + block, F32),
        pltpu.VMEM((2, 2, NZ, TILE, 128), F32),
        pltpu.VMEM((2, TILE, 128), F32),
        pltpu.VMEM((2, NC, NX) + block, BF16),
        pltpu.VMEM((2, NC, NX) + block, BF16),
        pltpu.VMEM((2, NY, rows // 2 + 8, 128), F32),
        pltpu.VMEM((5, NX * NC, 4, 128), F32),
        pltpu.VMEM((5, NZ, 4, 128), F32),
        pltpu.VMEM((NC, rows, columns // NC), BF16),
        pltpu.VMEM((columns, 128), F32),
        dma((6,)),
        dma((2,)), dma((2, NX)),
        dma((2,)), dma((2, 2)),
        dma((2,)), dma((2,)),
        dma((2, tiles - NZ)), dma((2,)),
        dma((4,)), dma((4, 2)),
        dma((4,)), dma((4, tiles - NZ)),
        dma((4,)), dma((4, 2, NX)),
        dma((4,)), dma((4,)),
        dma((2,)), dma((2,)),
        dma((5,)), dma((5,)),
        dma((5,)), dma((5,)),
    ]
    return pl.pallas_call(
        kernel,
        out_shape=jax.ShapeDtypeStruct((columns, 128), F32),
        in_specs=[hbm] * 5,
        out_specs=vmem,
        scratch_shapes=scratch,
        compiler_params=pltpu.CompilerParams(
            collective_id=0, has_side_effects=True, vmem_limit_bytes=63 * 1024 * 1024
        ),
    )(design, observed.T, arc_lengths, arc_months, walk_weight)


def solution(mesh):
    in_specs = (P("arcs", "coef"), P("arcs", None), P("arcs", None), P("arcs", None), P("coef"))
    return jax.shard_map(
        body, mesh=mesh, in_specs=in_specs, out_specs=P("coef", None), check_vma=False
    )
```

```python
import functools

import jax
import jax.numpy as jnp
from jax import lax
from jax.experimental import pallas as pl
from jax.experimental.pallas import tpu as pltpu
from jax.sharding import PartitionSpec as P

NCOEF = 9405
EPS = 1e-06
MESH = pl.DeviceIdType.MESH
NX, NZ, NC, NY = 4, 16, 2, 4
TILE = 16
SPLIT = 10
F32, BF16 = jnp.float32, jnp.bfloat16


def kernel(
    design, observed, lengths, months, walk, first_out, second_out, weight1_out, weight2_out,
    d_ref, dt, ob_ref, len_ref, mon_ref, walk_ref, wt, mask_ref, u_ref, bc_ref,
    cs, cr, xs, xr, tb, zr, own, vh, vl, yb, ng, nz, d2, joined,
    in_sem, cs_s, cs_r, xs_s, xs_r, zs_s, zs_r, ze_s, ze_r,
    az_s, az_r, ae_s, ae_r, ax_s, ax_r, ac_s, ac_r, y_s, y_r,
    ng_s, ng_r, nz_s, nz_r, out_s,
):
    rows = d_ref.shape[0]
    columns = d_ref.shape[1]
    tiles = columns // (NC * NX * TILE)
    piece = tiles * TILE
    extras = tiles - NZ
    halves = (pl.ds(0, SPLIT), pl.ds(SPLIT, tiles - SPLIT))
    both = pl.ds(0, tiles)
    arc, y = lax.axis_index("arcs"), lax.axis_index("coef")
    core = lax.rem(arc, NC)
    z = lax.rem(arc // NC, NZ)
    x = arc // (NC * NZ)

    def at(x_, z_, c_):
        return ((x_ * NZ + z_) * NC + c_, y)

    def wrap(v, n):
        return lax.rem(v, n)

    sibling = at(x, z, 1 - core)
    hops4 = (2, 1, 3)

    def x_peer(d):
        return wrap(x + d, NX)

    def y_peer(d):
        return (arc, wrap(y + d, NY))

    def extra_owner(e, c_):
        return 3 * e + c_

    drains = []

    def push(src, dst, ssem, rsem, dev):
        return pltpu.make_async_remote_copy(
            src_ref=src, dst_ref=dst, send_sem=ssem, recv_sem=rsem,
            device_id=dev, device_id_type=MESH,
        )

    def sent(ref, sem):
        drains.append(push(ref, ref, sem, sem, sibling).wait_send)

    def received(ref, sem):
        push(ref, ref, sem, sem, sibling).wait_recv()

    def nth(i, middle):
        return middle + lax.div(i + 1, 2) * (1 - 2 * lax.rem(i, 2))

    def loop(count, body):
        def step(i, _):
            body(i)
            return 0
        lax.fori_loop(0, count, step, 0)

    def over_z(body):
        loop(NZ - 1, lambda i: body(wrap(z + nth(i, NZ // 2), NZ)))

    def over_x(body):
        loop(NX - 1, lambda i: body(wrap(x + nth(i, NX // 2), NX)))

    barrier = pltpu.get_barrier_semaphore()

    def greet(dev):
        pl.semaphore_signal(barrier, inc=1, device_id=dev, device_id_type=MESH)

    over_z(lambda z_: greet(at(x, z_, core)))
    for d in hops4:
        greet(at(x_peer(d), z, core))
        greet(at(x_peer(d), z, 1 - core))
        greet(y_peer(d))
    greet(sibling)

    has_extra = jnp.int32(0)
    which = jnp.int32(0)
    for e in range(extras):
        hit = (z == extra_owner(e, core)).astype(jnp.int32)
        has_extra = has_extra + hit
        which = which + e * hit
    late = (z >= SPLIT).astype(jnp.int32)
    base = (core * NX + x) * piece
    firsts = [base + z * TILE, base + (NZ + which) * TILE]

    loads = [
        pltpu.make_async_copy(src, dst, in_sem.at[i])
        for i, (src, dst) in enumerate([
            (lengths, len_ref), (months, mon_ref), (observed, ob_ref), (design, d_ref),
        ] + [
            (walk.at[pl.ds(pl.multiple_of(f // 128 * 128, 128), 128)], walk_ref.at[s])
            for s, f in enumerate(firsts)
        ])
    ]
    for load in loads:
        load.start()

    lane = lax.broadcasted_iota(jnp.int32, (rows, 128), 1)
    row = lax.broadcasted_iota(jnp.int32, (rows, 128), 0)
    start = jnp.int32(0)
    month_row = jnp.full((rows, 128), -1, jnp.int32)
    loads[0].wait()
    loads[1].wait()
    for j in range(len_ref.shape[1]):
        end = start + len_ref[0, j]
        month_row = jnp.where((row >= start) & (row < end), mon_ref[0, j], month_row)
        start = end
    side = (lane >= 64).astype(jnp.int32)
    mask_stack = (month_row == side).astype(F32)
    mask_ref[...] = mask_stack
    half = rows // 2
    low = lax.broadcasted_iota(jnp.int32, (half, 128), 1) < 64
    loads[2].wait()
    ob = ob_ref[...].astype(F32)
    ob = jnp.concatenate([ob, ob], axis=0).T * mask_stack

    def turn(v):
        return pltpu.roll(v, 64, 1)

    def compact(v):
        s = v + turn(v)
        return jnp.where(low, s[:half], s[half:])

    def expand(v):
        t = turn(v)
        first = jnp.where(low, v, t)
        second = jnp.where(low, t, v)
        return (jnp.concatenate([first, second], axis=0) * mask_ref[...]).astype(BF16)

    def fold(v):
        return v + turn(jnp.broadcast_to(v, (8, 128)))[:1]

    def total(v):
        return jnp.sum(v, axis=0, keepdims=True)

    def padded(parts):
        rest = 4 - len(parts)
        if rest:
            parts = parts + [jnp.zeros((rest, 128), F32)]
        return jnp.concatenate(parts, axis=0)

    bc = compact(ob)
    bc_ref[...] = bc
    u_ref[0] = expand(bc)

    row16 = lax.broadcasted_iota(jnp.int32, (TILE, 128), 0)
    w_parts, keep_parts = [], []
    for s in range(2):
        first = firsts[s]
        inside = lax.rem(first, 128)
        loads[4 + s].wait()
        wt[s] = jnp.broadcast_to(walk_ref[s:s + 1, :], (128, 128)).T
        w_parts.append(wt[s, pl.ds(pl.multiple_of(inside, TILE), TILE), :])
        keep = (y * columns + first + row16) < NCOEF
        if s == 1:
            keep = keep & (jnp.full((TILE, 128), has_extra, jnp.int32) > 0)
        keep_parts.append(keep.astype(F32))

    loads[3].wait()
    for j in range(columns // 128):
        dt[j * 128:(j + 1) * 128, :] = d_ref[:, j * 128:(j + 1) * 128].T
    for c_ in range(NC):
        d2[c_] = d_ref[:, c_ * (columns // NC):(c_ + 1) * (columns // NC)]

    def adjoint_piece(r, h, p):
        first = pl.multiple_of((h * NX + p) * piece, TILE)
        value = jnp.dot(dt[pl.ds(first, piece), :], u_ref[r], preferred_element_type=F32)
        return value.reshape(tiles, TILE, 128)

    pl.semaphore_wait(barrier, 1 + 3 * len(hops4) + NZ - 1)

    def n_group(k, value):
        slot = x * NC + core
        ng[k, slot] = value

        def give(x_, c_):
            push(ng.at[k, slot], ng.at[k, slot], ng_s.at[k], ng_r.at[k], at(x_, z, c_)).start()

        def give_both(x_):
            give(x_, core)
            give(x_, 1 - core)
        over_x(give_both)
        give(x, 1 - core)
        sent(ng.at[k, pl.ds(0, NX * NC - 1)], ng_s.at[k])

    def n_group_sum(k):
        received(ng.at[k, pl.ds(0, NX * NC - 1)], ng_r.at[k])
        return jnp.sum(ng[k], axis=0)

    def n_z(k, value):
        nz[k, z] = value
        over_z(lambda z_: push(nz.at[k, z], nz.at[k, z], nz_s.at[k], nz_r.at[k], at(x, z_, core)).start())
        sent(nz.at[k, pl.ds(0, NZ - 1)], nz_s.at[k])

    def n_z_sum(k):
        received(nz.at[k, pl.ds(0, NZ - 1)], nz_r.at[k])
        return jnp.sum(nz[k], axis=0)

    def reduce_scatter(r, k, norm_value):
        n_group(k, norm_value)

        def theirs(i):
            p = wrap(x + nth(i, NX // 2), NX)
            cs[r, p] = adjoint_piece(r, 1 - core, p)
            push(cs.at[r, p], cr.at[r, p], cs_s.at[r], cs_r.at[r, p], sibling).start()
        loop(NX, theirs)
        sent(cs.at[r], cs_s.at[r])

        def mine(p):
            value = adjoint_piece(r, core, p)
            received(cr.at[r, p], cs_r.at[r, p])
            return value + cr[r, p]

        def away(p):
            xs[r, p] = mine(p)
            half_away(p, 0)

        def half_away(p, h):
            push(xs.at[r, p, halves[h]], xr.at[r, x, halves[h]], xs_s.at[r], xs_r.at[r, h], at(p, z, core)).start()
        over_x(away)
        over_x(lambda p: half_away(p, 1))
        sent(xs.at[r, pl.ds(0, NX - 1)], xs_s.at[r])
        n_z(k, n_group_sum(k))
        xr[r, x] = mine(x)

        def elsewhere(e, act):
            pl.when(z != extra_owner(e, core))(act)

        for h in range(2):
            part = halves[h]
            received(xr.at[r, pl.ds(0, NX - 1), part], xs_r.at[r, h])
            tb[r, part] = (xr[r, 0, part] + xr[r, 1, part]) + (xr[r, 2, part] + xr[r, 3, part])
            if h == 1:
                for e in range(extras):
                    elsewhere(e, lambda e=e: push(
                        tb.at[r, NZ + e], zr.at[r, 1, z], ze_s.at[r, e], ze_r.at[r],
                        at(x, extra_owner(e, core), core)).start())

            def out_tile(z_, h=h):
                @pl.when((z_ >= SPLIT) if h else (z_ < SPLIT))
                def _():
                    push(tb.at[r, z_], zr.at[r, 0, z], zs_s.at[r], zs_r.at[r], at(x, z_, core)).start()
            over_z(out_tile)
        sent(tb.at[r, pl.ds(0, NZ - 1)], zs_s.at[r])
        zr[r, 0, z] = tb[r, z]

        def drain():
            for e in range(extras):
                elsewhere(e, lambda e=e: push(
                    tb.at[r, 0], tb.at[r, 0], ze_s.at[r, e], ze_s.at[r, e], sibling).wait_send())
        drains.append(drain)
        return n_z_sum(k)

    def owned(r, s):
        if s == 0:
            received(zr.at[r, 0, pl.ds(0, NZ - 1)], zs_r.at[r])
            return jnp.sum(zr[r, 0], axis=0) * keep_parts[0]
        own[r] = jnp.zeros((TILE, 128), F32)

        @pl.when(has_extra > 0)
        def _():
            zr[r, 1, z] = tb[r, NZ + which]
            received(zr.at[r, 1, pl.ds(0, NZ - 1)], ze_r.at[r])
            own[r] = jnp.sum(zr[r, 1], axis=0)
        return own[r] * keep_parts[1]

    def keep_tile(v, r, s, value):
        if s == 0:
            v[r, core, x, z] = value
        else:
            @pl.when(has_extra > 0)
            def _():
                v[r, core, x, NZ + which] = value

    def publish(v, r, q, s):
        many = v.at[r, core, x, pl.ds(0, NZ - 1)]
        if s == 0:
            main = v.at[r, core, x, z]
            over_z(lambda z_: push(main, main, az_s.at[q], az_r.at[q, late], at(x, z_, core)).start())
            sent(many, az_s.at[q])
            return

        @pl.when(has_extra > 0)
        def _():
            ref = v.at[r, core, x, NZ + which]
            over_z(lambda z_: push(ref, ref, ae_s.at[q], ae_r.at[q, which], at(x, z_, core)).start())

        def drain():
            @pl.when(has_extra > 0)
            def _():
                push(many, many, ae_s.at[q], ae_s.at[q], sibling).wait_send()
        drains.append(drain)

    def tiles_wait(v, r, q, h):
        count = NZ - SPLIT if h else SPLIT
        for inside in range(2):
            @pl.when(late == (h if inside else 1 - h))
            def _():
                received(v.at[r, core, x, pl.ds(0, count - inside)], az_r.at[q, h])
        if h == 1:
            for e in range(extras):
                @pl.when(z != extra_owner(e, core))
                def _():
                    received(v.at[r, core, x, 0], ae_r.at[q, e])

    def to_sibling(v, r, q, p, part):
        ref = v.at[r, core, p, part]
        push(ref, ref, ac_s.at[q], ac_r.at[q], sibling).start()

    def gather_x_start(v, r, q, part, h):
        ref = v.at[r, core, x, part]
        over_x(lambda x_: push(ref, ref, ax_s.at[q], ax_r.at[q, h, x], at(x_, z, core)).start())
        sent(v.at[r, core, pl.ds(0, NX - 1), part], ax_s.at[q])
        to_sibling(v, r, q, x, part)

    def gather_x_forward(v, r, q, part, h):
        for d in (1, 3, 2):
            p = x_peer(d)
            received(v.at[r, core, p, part], ax_r.at[q, h, p])
            to_sibling(v, r, q, p, part)
        sent(v.at[r, core, pl.ds(0, NX), part], ac_s.at[q])

    def gather_core_wait(v, r, q):
        received(v.at[r, 1 - core], ac_r.at[q])

    def rest_wait(r):
        for h in range(2):
            tiles_wait(vl, r, 2 * r + 1, h)

    def forward(r, c_):
        value = vh[r, c_].reshape(columns // NC, 128)
        return jnp.dot(d2[c_], value, preferred_element_type=F32)

    def y_start(r, partial, norms):
        yb[r, y, :half] = partial
        yb[r, y, half:half + 8] = jnp.concatenate([norms, jnp.zeros((4, 128), F32)], axis=0)
        for d in hops4:
            push(yb.at[r, y], yb.at[r, y], y_s.at[r], y_r.at[r], y_peer(d)).start()
        sent(yb.at[r, pl.ds(0, NY - 1)], y_s.at[r])

    def y_wait(r):
        received(yb.at[r, pl.ds(0, NY - 1)], y_r.at[r])
        value = (yb[r, 0] + yb[r, 1]) + (yb[r, 2] + yb[r, 3])
        return value[:half], value[half:half + 4]

    def split(value):
        hi = value.astype(BF16)
        return hi, (value - hi.astype(F32)).astype(BF16)

    def gather(r, k, make, norms_of):
        values = []
        for s in range(2):
            value = make(s, owned(r, s))
            hi, lo = split(value)
            keep_tile(vh, r, s, hi)
            publish(vh, r, 2 * r, s)
            keep_tile(vl, r, s, lo)
            values.append(value)
        n_z(k, norms_of(values))
        for h in range(2):
            tiles_wait(vh, r, 2 * r, h)
            gather_x_start(vh, r, 2 * r, halves[h], h)
        n_group(k, n_z_sum(k))
        for s in range(2):
            publish(vl, r, 2 * r + 1, s)
        for h in range(2):
            gather_x_forward(vh, r, 2 * r, halves[h], h)
        image = forward(r, core)
        gather_core_wait(vh, r, 2 * r)
        image = image + forward(r, 1 - core)
        y_start(r, compact(image * mask_ref[...]), n_group_sum(k))
        rest_wait(r)
        gather_x_start(vl, r, 2 * r + 1, both, 0)
        return values

    def root(v):
        return jnp.sqrt(v + EPS)

    def walk_of(s, v):
        return w_parts[s] * (turn(v) - v)

    def totals(parts):
        return total(parts[0]) + total(parts[1])

    norm = reduce_scatter(0, 0, padded([total(bc * bc)]))
    beta1 = root(fold(norm[0:1]))

    def norms1(v):
        dv8 = [walk_of(s, v[s]) * 0.125 for s in range(2)]
        return padded([totals([e * e for e in v]), totals([e * e for e in dv8])])

    v1 = gather(0, 1, lambda s, got: got / beta1, norms1)
    image, norms = y_wait(0)

    alpha1 = root(fold(norms[0:1]))
    o2 = image / alpha1 - alpha1 * (bc_ref[...] / beta1)
    u_ref[1] = expand(o2)
    walk2 = (norms[1:2] / (alpha1 * alpha1)) * 64.0
    norm = reduce_scatter(1, 2, padded([total(o2 * o2)]))
    beta2 = jnp.sqrt(fold(norm[0:1]) + walk2 + EPS)
    wz = [(walk_of(s, v1[s]) / alpha1) / beta2 for s in range(2)]

    def second_vector(s, got):
        return got / beta2 - w_parts[s] * wz[s] - beta2 * (v1[s] / alpha1)

    def norms2(v):
        dv8 = [walk_of(s, v[s]) * 0.125 for s in range(2)]
        return padded([
            totals([e * e for e in v]),
            totals([e * e for e in dv8]),
            totals([e * g for e, g in zip(dv8, wz)]),
            totals([g * g for g in wz]),
        ])

    v2 = gather(1, 3, second_vector, norms2)
    gather_x_forward(vl, 0, 1, both, 0)
    image, norms = y_wait(1)

    alpha2 = root(fold(norms[0:1]))
    o3 = image / alpha2 - alpha2 * (o2 / beta2)
    n_group(4, padded([total(o3 * o3)]))
    square = alpha2 * alpha2
    walk3 = (norms[1:2] / square) * 64.0 - 16.0 * norms[2:3] + square * norms[3:4]
    walk3 = jnp.maximum(walk3, 0.0)
    n_z(4, n_group_sum(4))
    gather_x_forward(vl, 1, 3, both, 0)
    rho1 = jnp.sqrt(alpha1 * alpha1 + beta2 * beta2)
    cos1, sin1 = alpha1 / rho1, beta2 / rho1
    first_step = cos1 * beta1 / rho1
    phi_bar = sin1 * beta1
    rho_bar = -cos1 * alpha2
    theta = sin1 * alpha2 / rho1
    gather_core_wait(vl, 0, 1)
    gather_core_wait(vl, 1, 3)
    for c_ in range(NC):
        for p in range(NX):
            begin = (c_ * NX + p) * piece
            for r in range(2):
                value = vh[r, c_, p].astype(F32) + vl[r, c_, p].astype(F32)
                joined[r, begin:begin + piece, :] = value.reshape(piece, 128)
    stores = [
        pltpu.make_async_copy(joined.at[r], target, out_s.at[r])
        for r, target in enumerate((first_out, second_out))
    ]
    for store in stores:
        store.start()
    beta3 = jnp.sqrt(fold(n_z_sum(4)[0:1]) + walk3 + EPS)
    rho2 = jnp.sqrt(rho_bar * rho_bar + beta3 * beta3)
    second_step = (rho_bar / rho2) * phi_bar / rho2
    weight1 = (first_step - second_step * theta) / alpha1
    weight2 = second_step / alpha2
    weight1_out[...] = weight1
    weight2_out[...] = weight2
    for store in stores:
        store.wait()

    for drain in drains:
        drain()


def body(design, observed, arc_lengths, arc_months, walk_weight):
    rows, columns = design.shape
    tiles = columns // (NC * NX * TILE)
    vmem = pl.BlockSpec(memory_space=pltpu.VMEM)
    hbm = pl.BlockSpec(memory_space=pltpu.HBM)
    dma = pltpu.SemaphoreType.DMA
    block = (tiles, TILE, 128)
    scratch = [
        pltpu.VMEM((rows, columns), BF16),
        pltpu.VMEM((columns, rows), BF16),
        pltpu.VMEM((observed.shape[1], rows), BF16),
        pltpu.SMEM(arc_lengths.shape, jnp.int32),
        pltpu.SMEM(arc_months.shape, jnp.int32),
        pltpu.VMEM((2, 128), F32),
        pltpu.VMEM((2, 128, 128), F32),
        pltpu.VMEM((rows, 128), F32),
        pltpu.VMEM((2, rows, 128), BF16),
        pltpu.VMEM((rows // 2, 128), F32),
        pltpu.VMEM((2, NX) + block, F32),
        pltpu.VMEM((2, NX) + block, F32),
        pltpu.VMEM((2, NX) + block, F32),
        pltpu.VMEM((2, NX) + block, F32),
        pltpu.VMEM((2,) + block, F32),
        pltpu.VMEM((2, 2, NZ, TILE, 128), F32),
        pltpu.VMEM((2, TILE, 128), F32),
        pltpu.VMEM((2, NC, NX) + block, BF16),
        pltpu.VMEM((2, NC, NX) + block, BF16),
        pltpu.VMEM((2, NY, rows // 2 + 8, 128), F32),
        pltpu.VMEM((5, NX * NC, 4, 128), F32),
        pltpu.VMEM((5, NZ, 4, 128), F32),
        pltpu.VMEM((NC, rows, columns // NC), BF16),
        pltpu.VMEM((2, columns, 128), F32),
        dma((6,)),
        dma((2,)), dma((2, NX)),
        dma((2,)), dma((2, 2)),
        dma((2,)), dma((2,)),
        dma((2, tiles - NZ)), dma((2,)),
        dma((4,)), dma((4, 2)),
        dma((4,)), dma((4, tiles - NZ)),
        dma((4,)), dma((4, 2, NX)),
        dma((4,)), dma((4,)),
        dma((2,)), dma((2,)),
        dma((5,)), dma((5,)),
        dma((5,)), dma((5,)),
        dma((2,)),
    ]
    vector = jax.ShapeDtypeStruct((columns, 128), F32)
    weight = jax.ShapeDtypeStruct((1, 128), F32)
    first, second, weight1, weight2 = pl.pallas_call(
        kernel,
        out_shape=[vector, vector, weight, weight],
        in_specs=[hbm] * 5,
        out_specs=[hbm, hbm, vmem, vmem],
        scratch_shapes=scratch,
        compiler_params=pltpu.CompilerParams(
            collective_id=0, has_side_effects=True, vmem_limit_bytes=63 * 1024 * 1024
        ),
    )(design, observed.T, arc_lengths, arc_months, walk_weight)
    return weight1 * first + weight2 * second


def solution(mesh):
    in_specs = (P("arcs", "coef"), P("arcs", None), P("arcs", None), P("arcs", None), P("coef"))
    return jax.shard_map(
        body, mesh=mesh, in_specs=in_specs, out_specs=P("coef", None), check_vma=False
    )
```
